256 devices in a mesh: mp: 8 (over z_lo, core), dp: 8 (over z_hi, y), shard: 4 (over x).
Axes of the slice: x: 4, y: 4, z: 8 (z_hi: 2, z_lo: 4; z = z_hi * 4 + z_lo), core: 2. Of those that a mesh axis runs over, the one named last changes fastest.
Arguments:
- hidden: bfloat16 [8, 1024, 4096], P('mp', 'dp', 'shard'), may hold values from -6 to 6
- cotangent: bfloat16 [8, 1024, 14336], P('mp', 'dp', 'shard'), may hold values from -6 to 6
- weights: bfloat16 [8, 4096, 14336], P('mp', 'dp', 'shard'), may hold values from -6 to 6
- segments: int32 [8, 128], replicated, may hold values from 0 to 2, never falling along the last dimension, each value on 1 to 64 neighbouring positions
Outputs:
- merged: bfloat16 [4096, 14336], P(('dp', 'mp'), 'shard')
The draws below stay inside these ranges and needn't reach their ends.
Inputs may be any that keep to these rules, and one draw needn't show every extreme that they name: `segments`: in every row the numbers never fall, each of the 3 numbers covers 1 to 64 tokens, and one covers exactly 64.
All inputs are finite; a program needn't handle non-finite values.
Results may differ from the reference program's by a relative error of at most 0.015.
Values may be sent and summed in bfloat16 or wider, within the bound.
A program may use at most 128 MiB of HBM per device.

```python
import math
import jax
import jax.numpy as jnp
import numpy as np
from jax import lax

D = 4096
F = 14336
TOK_DEV = 128
EX = 3
LONGEST = 64
MODELS = 8
TOKENS = 1024
N_DP = 8


def block_levels(own_key, dims, split, low, top_value):
    level = 1.0
    for dim, blocks in split:
        draws = jax.random.uniform(jax.random.fold_in(jax.random.fold_in(own_key, 6), dim), (blocks,), jnp.float32, low / len(split), top_value / len(split))
        level = level * jnp.repeat(jnp.exp(draws), dims[dim] // blocks).reshape((-1,) + (1,) * (len(dims) - 1 - dim))
    return level


def length_profile(count, total, limit, skew):
    loads = [(1 << 20) // math.isqrt(standing ** skew) + 1 for standing in range(2, count + 1)]
    surplus, given = total - limit - (count - 1), [1] * (count - 1)
    while surplus > 0:
        movable = [i for i in range(count - 1) if given[i] < limit]
        mass, budget = sum([loads[i] for i in movable]), surplus
        for i in movable:
            more = min(limit - given[i], max(1, budget * loads[i] // mass), surplus)
            given[i] = given[i] + more
            surplus = surplus - more
    return np.array([limit] + given)


def ragged(rng, count, total, reach, skew):
    if count == 2:
        one = jax.random.randint(rng, (), max(1, total - reach), min(reach, total - 1) + 1)
        return jnp.stack([one, total - one])
    tallies = jnp.asarray(length_profile(count, total, reach, skew), jnp.int32)
    couples = (count - 1) // 2
    giver, receiver = tallies[1:1 + 2 * couples:2], tallies[2:2 + 2 * couples:2]
    slack = jnp.minimum(giver - 1, reach - receiver)
    moved = jax.random.randint(jax.random.fold_in(rng, 1), (couples,), 0, 1 << 20) % (slack + 1)
    tallies = tallies.at[1:1 + 2 * couples:2].set(giver - moved).at[2:2 + 2 * couples:2].set(receiver + moved)
    return tallies[jax.random.permutation(jax.random.fold_in(rng, 2), count)]


def scatter_about(key, dims, spread, reach, split=(), held_as=jnp.bfloat16):
    drawn = jax.random.normal(key, dims, jnp.float32) * spread
    if len(split) > 0:
        drawn = block_levels(key, dims, split, -0.22, 0.18) * drawn
    return jnp.clip(drawn, min=-reach, max=reach).astype(held_as)


def setup_inputs(seed: int = 0) -> dict:
    streams_of = jax.random.split(jax.random.key(seed), 5)
    return {
        "hidden": scatter_about(streams_of[0], (MODELS, TOKENS, D), 1.0, 6.0, ((0, 8), (1, 8), (2, 4))),
        "cotangent": scatter_about(streams_of[1], (MODELS, TOKENS, F), 1.0, 6.0, ((0, 8), (1, 8), (2, 4))),
        "weights": scatter_about(streams_of[2], (MODELS, D, F), 1.0, 6.0, ((0, 8), (1, 8), (2, 4))),
        "segments": jax.vmap(lambda own: jnp.searchsorted(jnp.cumsum(ragged(own, EX, TOK_DEV, LONGEST, 2)), jnp.arange(TOK_DEV), side="right"))(jax.random.split(streams_of[3], N_DP)).reshape((N_DP, TOK_DEV)).astype(jnp.int32),
    }


def example_rows(segments):
    labels = jnp.arange(EX, dtype=jnp.int32)
    starts = lax.optimization_barrier(jnp.sum((segments[:, None, :] < labels[None, :, None]).astype(jnp.int32), axis=2))
    counts = lax.optimization_barrier(jnp.sum((segments[:, None, :] == labels[None, :, None]).astype(jnp.int32), axis=2))
    offsets = jnp.arange(LONGEST, dtype=jnp.int32)
    local = starts[:, :, None] + offsets[None, None, :]
    valid = offsets[None, None, :] < counts[:, :, None]
    return (local, valid)

def reference(hidden, cotangent, weights, segments):
    block_rows = D // N_DP
    inv_root = 1.0 / math.sqrt(D)
    local, valid = example_rows(segments)
    base = (jnp.arange(N_DP, dtype=jnp.int32) * TOK_DEV)[:, None, None]
    rows_all = jnp.minimum(local + base, TOKENS - 1).astype(jnp.int32).reshape(N_DP * EX, LONGEST)
    valid_all = valid.reshape(N_DP * EX, LONGEST)

    def one_model(carry, inputs):
        numer, denom = carry
        states, cotan, weight = inputs

        def add_block(total, number):
            cols = lax.dynamic_slice_in_dim(states, number * block_rows, block_rows, 1)
            rows = lax.dynamic_slice_in_dim(weight, number * block_rows, block_rows, 0)
            part = jnp.dot(cols, rows, preferred_element_type=jnp.float32).astype(jnp.bfloat16)
            return (total + lax.optimization_barrier(part).astype(jnp.float32), None)
        summed, _ = lax.scan(add_block, jnp.zeros((TOKENS, F), jnp.float32), jnp.arange(N_DP, dtype=jnp.int32))
        pre = summed * inv_root
        sig = jax.nn.sigmoid(pre)
        outgrad = (cotan.astype(jnp.float32) * sig * (1.0 + pre * (1.0 - sig))).astype(jnp.bfloat16)

        def add_example(fisher, picked):
            rows, keep = picked
            taken = jnp.take(states, rows, axis=0)
            grads_out = jnp.where(keep[:, None], jnp.take(outgrad, rows, axis=0), jnp.zeros((), jnp.bfloat16))
            grad = jnp.dot(taken.T, grads_out, preferred_element_type=jnp.float32).astype(jnp.bfloat16)
            grad = lax.optimization_barrier(grad).astype(jnp.float32)
            return (fisher + grad * grad, None)
        fisher, _ = lax.scan(add_example, jnp.zeros((D, F), jnp.float32), (rows_all, valid_all))
        return ((numer + fisher * weight.astype(jnp.float32), denom + fisher), None)
    start_sums = (jnp.zeros((D, F), jnp.float32), jnp.zeros((D, F), jnp.float32))
    (numer, denom), _ = lax.scan(one_model, start_sums, (hidden, cotangent, weights))
    return (numer / denom).astype(jnp.bfloat16)
```

```python
import math

import jax
import jax.numpy as jnp
from jax import lax
from jax.experimental import pallas as pl
from jax.experimental.pallas import tpu as pltpu
from jax.sharding import PartitionSpec as P

EX = 3
Y = 4
CHUNK = 256
ROWS_AT_ONCE = 64
LAG_SUM, LAG_GRAD, LAG_PASS, LAG_FISHER, LAG_CORE, LAG_NEAR, LAG_FAR = 1, 2, 3, 4, 5, 6, 7


def kernel(
    hidden, cotangent, weights, segments, out,
    w, cot, states, masked, part, part_in, own, cross, cross_in, grads, sums,
    core_in, near_in, far_in, result, fisher,
    load_sem, hid_ssem, hid_rsem, x_ssem, x_rsem, out_sem,
    part_ssem, part_rsem, cross_ssem, cross_rsem, gz_ssem, gz_rsem, gy_ssem, gy_rsem, gf_ssem, gf_rsem,
    core_ssem, core_rsem, near_ssem, near_rsem, far_ssem, far_rsem,
):
    chunks, block_rows, cw = w.shape
    tokens = cot.shape[1]
    quarter = tokens // Y
    scale = 1.0 / math.sqrt(block_rows * 2 * Y)
    mp, dp, sh = lax.axis_index("mp"), lax.axis_index("dp"), lax.axis_index("shard")
    core, b0, b1 = lax.rem(mp, 2), lax.rem(mp // 2, 2), mp // 4
    zh, y = dp // Y, lax.rem(dp, Y)

    def y_peer(d):
        return {"dp": zh * Y + lax.rem(y + d, Y)}

    def x_peer(d):
        return {"shard": lax.rem(sh + d, Y)}

    z_peer = {"dp": (1 - zh) * Y + y}
    core_peer = {"mp": mp + 1 - 2 * core}
    near_peer = {"mp": mp + 2 - 4 * b0}
    far_peer = {"mp": mp + 4 - 8 * b1}

    def remote(src, dst, ssem, rsem, device):
        return pltpu.make_async_remote_copy(
            src_ref=src,
            dst_ref=dst,
            send_sem=ssem,
            recv_sem=rsem,
            device_id=device,
            device_id_type=pl.DeviceIdType.MESH,
        )

    def load_w(c):
        cols = pl.ds(pl.multiple_of(c * cw, cw), cw)
        return pltpu.make_async_copy(weights.at[0, :, cols], w.at[c], load_sem.at[c])

    def load_cot(c):
        cols = pl.ds(pl.multiple_of(c * cw, cw), cw)
        return pltpu.make_async_copy(
            cotangent.at[0, :, cols], cot.at[c], load_sem.at[chunks + c]
        )

    def start_loads(c, carry):
        load_w(c).start()
        load_cot(c).start()
        return carry

    lax.fori_loop(0, chunks, start_loads, 0)

    barrier = pltpu.get_barrier_semaphore()

    def greet(device):
        pl.semaphore_signal(
            barrier, inc=1, device_id=device, device_id_type=pl.DeviceIdType.MESH
        )

    def from_self(j):
        return jnp.logical_and(sh == dp // 2, dp == j)

    def to_self(b, q):
        return jnp.logical_and(dp == 2 * sh + b, sh == q)

    peers = [y_peer(1), y_peer(2), y_peer(3), x_peer(1), x_peer(2), x_peer(3)]
    peers += [z_peer, core_peer, near_peer, far_peer]
    for device in peers:
        greet(device)
    for j in range(2 * Y):

        @pl.when(jnp.logical_not(from_self(j)))
        def _():
            greet({"dp": j, "shard": dp // 2})

    at_home = jnp.where(sh == dp // 2, 1, 0)
    pl.semaphore_wait(barrier, len(peers) + 2 * Y - at_home)

    def hid_send(b, q):
        return remote(
            hidden.at[0, pl.ds(q * quarter, quarter), pl.ds(b * block_rows, block_rows)],
            states.at[dp, q],
            hid_ssem.at[b * Y + q],
            hid_rsem.at[dp],
            {"dp": 2 * sh + b, "shard": q},
        )

    def hid_local(b, q):
        return pltpu.make_async_copy(
            hidden.at[0, pl.ds(q * quarter, quarter), pl.ds(b * block_rows, block_rows)],
            states.at[dp, q],
            hid_ssem.at[b * Y + q],
        )

    def hid_recv(j):
        return remote(
            states.at[j, sh], states.at[j, sh], hid_ssem.at[0], hid_rsem.at[j], {"dp": j, "shard": dp // 2}
        )

    for b in range(2):
        for q in range(Y):

            @pl.when(to_self(b, q))
            def _():
                hid_local(b, q).start()

            @pl.when(jnp.logical_not(to_self(b, q)))
            def _():
                hid_send(b, q).start()

    for j in range(2 * Y):

        @pl.when(jnp.logical_not(from_self(j)))
        def _():
            hid_recv(j).wait_recv()

    for b in range(2):
        for q in range(Y):

            @pl.when(to_self(b, q))
            def _():
                hid_local(b, q).wait()

            @pl.when(jnp.logical_not(to_self(b, q)))
            def _():
                hid_send(b, q).wait_send()

    def x_send(d):
        return remote(
            states.at[:, sh], states.at[:, sh], x_ssem.at[d - 1], x_rsem.at[d - 1], x_peer(d)
        )

    def x_recv(d):
        place = states.at[:, lax.rem(sh - d + Y, Y)]
        return remote(place, place, x_ssem.at[d - 1], x_rsem.at[d - 1], x_peer(d))

    for d in range(1, Y):
        x_send(d).start()
    for d in range(1, Y):
        x_recv(d).wait_recv()
    for d in range(1, Y):
        x_send(d).wait_send()

    def part_send(c, d):
        return remote(
            part.at[c, :, lax.rem(y + d, Y)], part_in.at[c, d - 1],
            part_ssem.at[c, d - 1], part_rsem.at[c, d - 1], y_peer(d),
        )

    def cross_send(c):
        return remote(cross.at[c], cross_in.at[c], cross_ssem.at[c], cross_rsem.at[c], z_peer)

    def gz_send(c):
        place = grads.at[c, zh, y]
        return remote(place, place, gz_ssem.at[c], gz_rsem.at[c], z_peer)

    def gz_recv(c):
        place = grads.at[c, 1 - zh, y]
        return remote(place, place, gz_ssem.at[c], gz_rsem.at[c], z_peer)

    def gy_send(c, d):
        place = grads.at[c, zh, y]
        return remote(place, place, gy_ssem.at[c, d - 1], gy_rsem.at[c, d - 1], y_peer(d))

    def gy_recv(c, d):
        place = grads.at[c, zh, lax.rem(y - d + Y, Y)]
        return remote(place, place, gy_ssem.at[c, d - 1], gy_rsem.at[c, d - 1], y_peer(d))

    def gf_send(c, d):
        place = grads.at[c, 1 - zh, y]
        return remote(place, place, gf_ssem.at[c, d - 1], gf_rsem.at[c, d - 1], y_peer(d))

    def gf_recv(c, d):
        place = grads.at[c, 1 - zh, lax.rem(y - d + Y, Y)]
        return remote(place, place, gf_ssem.at[c, d - 1], gf_rsem.at[c, d - 1], y_peer(d))

    def core_send(c):
        return remote(
            sums.at[c, 1 - core], core_in.at[c], core_ssem.at[c], core_rsem.at[c], core_peer
        )

    def near_send(c):
        return remote(
            sums.at[c, core, 1 - b0], near_in.at[c], near_ssem.at[c], near_rsem.at[c], near_peer
        )

    def far_send(c):
        return remote(
            sums.at[c, core, b0, 1 - b1], far_in.at[c], far_ssem.at[c], far_rsem.at[c], far_peer
        )

    def store(c):
        cols = pl.ds(pl.multiple_of(c * cw, cw), cw)
        return pltpu.make_async_copy(result.at[c], out.at[:, cols], out_sem.at[c])

    def product(c):
        load_w(c).wait()

        def some(j, carry):
            rows = states[j].reshape(tokens, block_rows)
            part[c, j // Y, lax.rem(j, Y)] = jnp.dot(
                rows, w[c], preferred_element_type=jnp.float32
            ).astype(jnp.bfloat16)
            return carry

        lax.fori_loop(0, 2 * Y, some, 0)
        for d in range(1, Y):
            part_send(c, d).start()

    def mask_states():
        def some(j, carry):
            rows = states[j].reshape(tokens, block_rows)
            turned = rows.astype(jnp.float32).T
            labels = segments[pl.ds(j, 1), :]
            for e in range(EX):
                masked[j * EX + e] = jnp.where(labels == e, turned, 0.0).astype(jnp.bfloat16)
            return carry

        lax.fori_loop(0, 2 * Y, some, 0)

    def add_up(c):
        for d in range(1, Y):
            part_send(c, d).wait_recv()

        def total(half):
            acc = part[c, half, y].astype(jnp.float32)
            for d in range(1, Y):
                acc += part_in[c, d - 1, half].astype(jnp.float32)
            return acc

        cross[c] = total(1 - zh).astype(jnp.bfloat16)
        cross_send(c).start()
        own[c] = total(zh)

    def gradient(c):
        load_cot(c).wait()
        cross_send(c).wait_recv()
        pre = (own[c] + cross_in[c].astype(jnp.float32)) * scale
        sig = jax.nn.sigmoid(pre)
        grads[c, zh, y] = (
            cot[c].astype(jnp.float32) * sig * (1.0 + pre * (1.0 - sig))
        ).astype(jnp.bfloat16)
        gz_send(c).start()
        for d in range(1, Y):
            gy_send(c, d).start()

    def pass_on(c):
        gz_recv(c).wait_recv()
        for d in range(1, Y):
            gf_send(c, d).start()

    def fishers(c):
        for d in range(1, Y):
            gy_recv(c, d).wait_recv()
            gf_recv(c, d).wait_recv()

        def some(r, carry):
            rows = pl.ds(pl.multiple_of(r * ROWS_AT_ONCE, ROWS_AT_ONCE), ROWS_AT_ONCE)
            acc = jnp.zeros((ROWS_AT_ONCE, cw), jnp.float32)
            for j in range(2 * Y):
                cols = grads[c, j // Y, j % Y]
                for e in range(EX):
                    grad = jnp.dot(
                        masked[j * EX + e, rows, :], cols, preferred_element_type=jnp.float32
                    )
                    acc += grad * grad
            fisher[rows, :] = acc
            return carry

        lax.fori_loop(0, block_rows // ROWS_AT_ONCE, some, 0)
        per = block_rows // 8
        for m in range(8):
            f = fisher[m * per : (m + 1) * per, :]
            at = sums.at[c, m % 2, (m // 2) % 2, m // 4]
            at[0] = (f * w[c, m * per : (m + 1) * per, :].astype(jnp.float32)).astype(jnp.bfloat16)
            at[1] = f.astype(jnp.bfloat16)
        core_send(c).start()

    def add_core(c):
        core_send(c).wait_recv()
        for i in (0, 1):
            side = b0 if i else 1 - b0
            sums[c, core, side] = (
                sums[c, core, side].astype(jnp.float32) + core_in[c, side].astype(jnp.float32)
            ).astype(jnp.bfloat16)
            if i == 0:
                near_send(c).start()

    def add_near(c):
        near_send(c).wait_recv()
        for i in (0, 1):
            side = b1 if i else 1 - b1
            sums[c, core, b0, side] = (
                sums[c, core, b0, side].astype(jnp.float32)
                + near_in[c, side].astype(jnp.float32)
            ).astype(jnp.bfloat16)
            if i == 0:
                far_send(c).start()

    def add_far(c):
        far_send(c).wait_recv()
        both = sums[c, core, b0, b1].astype(jnp.float32) + far_in[c].astype(jnp.float32)
        result[c] = (both[0] / both[1]).astype(jnp.bfloat16)
        store(c).start()

    stages = [
        (product, 0), (add_up, LAG_SUM), (gradient, LAG_GRAD), (pass_on, LAG_PASS),
        (fishers, LAG_FISHER), (add_core, LAG_CORE), (add_near, LAG_NEAR), (add_far, LAG_FAR),
    ]

    def step(t, carry):
        for stage, lag in stages:
            c = t - lag

            @pl.when(jnp.logical_and(c >= 0, c < chunks))
            def _():
                stage(c)

            if stage is product:

                @pl.when(t == 0)
                def _():
                    mask_states()

        return carry

    lax.fori_loop(0, chunks + LAG_FAR, step, 0)

    def finish(c, carry):
        for d in range(1, Y):
            part_send(c, d).wait_send()
            gy_send(c, d).wait_send()
            gf_send(c, d).wait_send()
        cross_send(c).wait_send()
        gz_send(c).wait_send()
        core_send(c).wait_send()
        near_send(c).wait_send()
        far_send(c).wait_send()
        store(c).wait()
        return carry

    lax.fori_loop(0, chunks, finish, 0)


def shards(hidden, cotangent, weights, segments):
    tokens, block_rows, columns = hidden.shape[1], weights.shape[1], weights.shape[2]
    cw = CHUNK
    n = columns // cw
    per = block_rows // 8
    bf, f32 = jnp.bfloat16, jnp.float32
    dma = pltpu.SemaphoreType.DMA
    buffers = [
        pltpu.VMEM((n, block_rows, cw), bf),
        pltpu.VMEM((n, tokens, cw), bf),
        pltpu.VMEM((2 * Y, Y, tokens // Y, block_rows), bf),
        pltpu.VMEM((2 * Y * EX, block_rows, tokens), bf),
        pltpu.VMEM((n, 2, Y, tokens, cw), bf),
        pltpu.VMEM((n, Y - 1, 2, tokens, cw), bf),
        pltpu.VMEM((n, tokens, cw), f32),
        pltpu.VMEM((n, tokens, cw), bf),
        pltpu.VMEM((n, tokens, cw), bf),
        pltpu.VMEM((n, 2, Y, tokens, cw), bf),
        pltpu.VMEM((n, 2, 2, 2, 2, per, cw), bf),
        pltpu.VMEM((n, 2, 2, 2, per, cw), bf),
        pltpu.VMEM((n, 2, 2, per, cw), bf),
        pltpu.VMEM((n, 2, per, cw), bf),
        pltpu.VMEM((n, per, cw), bf),
        pltpu.VMEM((block_rows, cw), f32),
    ]
    many = [dma((n, Y - 1))] * 2
    one = [dma((n,))] * 2
    sems = [dma((2 * n,)), dma((2 * Y,)), dma((2 * Y,)), dma((Y - 1,)), dma((Y - 1,)), dma((n,))]
    sems += many + one + one + many + many + one + one + one
    return pl.pallas_call(
        kernel,
        out_shape=jax.ShapeDtypeStruct((per, columns), bf),
        in_specs=[pl.BlockSpec(memory_space=pl.ANY)] * 3
        + [pl.BlockSpec(memory_space=pltpu.VMEM)],
        out_specs=pl.BlockSpec(memory_space=pl.ANY),
        scratch_shapes=buffers + sems,
        compiler_params=pltpu.CompilerParams(
            collective_id=0, has_side_effects=True, vmem_limit_bytes=60 * 2**20
        ),
    )(hidden, cotangent, weights, segments)


def solution(mesh):
    return jax.shard_map(
        shards,
        mesh=mesh,
        in_specs=(P("mp", "dp", "shard"), P("mp", "dp", "shard"), P("mp", "dp", "shard"), P()),
        out_specs=P(("dp", "mp"), "shard"),
        check_vma=False,
    )
```

```python
import math

import jax
import jax.numpy as jnp
from jax import lax
from jax.experimental import pallas as pl
from jax.experimental.pallas import tpu as pltpu
from jax.sharding import PartitionSpec as P

EX = 3
Y = 4
CHUNK = 256
ROWS_AT_ONCE = 64
LAG_HALF, LAG_SUM, LAG_GRAD, LAG_PASS, LAG_RELAY = 1, 2, 3, 4, 5
LAG_FISHER, LAG_CORE, LAG_NEAR, LAG_FAR = 6, 7, 8, 9


def kernel(
    hidden, cotangent, weights, segments, out,
    w, cot, states, masked, part, half_in, part_in, own, cross, cross_in, grads, sums,
    core_in, near_in, far_in, result, fisher,
    load_sem, hid_ssem, hid_rsem, x_ssem, x_rsem, out_sem,
    half_ssem, half_rsem, soon_ssem, soon_rsem, late_ssem, late_rsem, cross_ssem, cross_rsem,
    gz_ssem, gz_rsem, gy_ssem, gy_rsem, relay_ssem, relay_rsem,
    core_ssem, core_rsem, near_ssem, near_rsem, far_ssem, far_rsem,
):
    chunks, block_rows, cw = w.shape
    tokens = cot.shape[1]
    quarter = tokens // Y
    scale = 1.0 / math.sqrt(block_rows * 2 * Y)
    mp, dp, sh = lax.axis_index("mp"), lax.axis_index("dp"), lax.axis_index("shard")
    core, b0, b1 = lax.rem(mp, 2), lax.rem(mp // 2, 2), mp // 4
    zh, y = dp // Y, lax.rem(dp, Y)

    def y_peer(d):
        return {"dp": zh * Y + lax.rem(y + d, Y)}

    def x_peer(d):
        return {"shard": lax.rem(sh + d, Y)}

    z_peer = {"dp": (1 - zh) * Y + y}
    core_peer = {"mp": mp + 1 - 2 * core}
    near_peer = {"mp": mp + 2 - 4 * b0}
    far_peer = {"mp": mp + 4 - 8 * b1}

    def remote(src, dst, ssem, rsem, device):
        return pltpu.make_async_remote_copy(
            src_ref=src,
            dst_ref=dst,
            send_sem=ssem,
            recv_sem=rsem,
            device_id=device,
            device_id_type=pl.DeviceIdType.MESH,
        )

    def load_w(c):
        cols = pl.ds(pl.multiple_of(c * cw, cw), cw)
        return pltpu.make_async_copy(weights.at[0, :, cols], w.at[c], load_sem.at[c])

    def load_cot(c):
        cols = pl.ds(pl.multiple_of(c * cw, cw), cw)
        return pltpu.make_async_copy(
            cotangent.at[0, :, cols], cot.at[c], load_sem.at[chunks + c]
        )

    def start_loads(c, carry):
        load_w(c).start()
        load_cot(c).start()
        return carry

    lax.fori_loop(0, chunks, start_loads, 0)

    barrier = pltpu.get_barrier_semaphore()

    def greet(device):
        pl.semaphore_signal(
            barrier, inc=1, device_id=device, device_id_type=pl.DeviceIdType.MESH
        )

    def from_self(j):
        return jnp.logical_and(sh == dp // 2, dp == j)

    def to_self(b, q):
        return jnp.logical_and(dp == 2 * sh + b, sh == q)

    peers = [y_peer(1), y_peer(3), x_peer(1), x_peer(2), x_peer(3)]
    peers += [z_peer, core_peer, near_peer, far_peer]
    for device in peers:
        greet(device)
    for j in range(2 * Y):

        @pl.when(jnp.logical_not(from_self(j)))
        def _():
            greet({"dp": j, "shard": dp // 2})

    at_home = jnp.where(sh == dp // 2, 1, 0)
    pl.semaphore_wait(barrier, len(peers) + 2 * Y - at_home)

    def hid_send(b, q):
        return remote(
            hidden.at[0, pl.ds(q * quarter, quarter), pl.ds(b * block_rows, block_rows)],
            states.at[dp, q],
            hid_ssem.at[b * Y + q],
            hid_rsem.at[dp],
            {"dp": 2 * sh + b, "shard": q},
        )

    def hid_local(b, q):
        return pltpu.make_async_copy(
            hidden.at[0, pl.ds(q * quarter, quarter), pl.ds(b * block_rows, block_rows)],
            states.at[dp, q],
            hid_ssem.at[b * Y + q],
        )

    def hid_recv(j):
        return remote(
            states.at[j, sh], states.at[j, sh], hid_ssem.at[0], hid_rsem.at[j], {"dp": j, "shard": dp // 2}
        )

    for b in range(2):
        for q in range(Y):

            @pl.when(to_self(b, q))
            def _():
                hid_local(b, q).start()

            @pl.when(jnp.logical_not(to_self(b, q)))
            def _():
                hid_send(b, q).start()

    def x_send(side, d):
        place = states.at[pl.ds(side * Y, Y), sh]
        at = side * (Y - 1) + d - 1
        return remote(place, place, x_ssem.at[at], x_rsem.at[at], x_peer(d))

    def x_recv(side, d):
        place = states.at[pl.ds(side * Y, Y), lax.rem(sh - d + Y, Y)]
        at = side * (Y - 1) + d - 1
        return remote(place, place, x_ssem.at[at], x_rsem.at[at], x_peer(d))

    def x_forward(side):
        for i in range(Y):
            j = side * Y + i

            @pl.when(jnp.logical_not(from_self(j)))
            def _():
                hid_recv(j).wait_recv()

            @pl.when(from_self(j))
            def _():
                hid_local(lax.rem(dp, 2), sh).wait()

        for d in range(1, Y):
            x_send(side, d).start()

    x_forward(zh)
    x_forward(1 - zh)
    for side in (zh, 1 - zh):
        for d in range(1, Y):
            x_recv(side, d).wait_recv()

    half = tokens // 2

    def y_next(i):
        return lax.rem(y + (1, Y - 1)[i], Y)

    def y_to(i):
        return y_peer((1, Y - 1)[i])

    def half_send(c, i):
        return remote(
            part.at[c, :, lax.rem(y + 2, Y), pl.ds(i * half, half)], half_in.at[c, i],
            half_ssem.at[c, i], half_rsem.at[c, i], y_to(i),
        )

    def soon_send(c, i):
        rows = pl.ds((1 - i) * half, half)
        return remote(
            part.at[c, :, y_next(i), rows], part_in.at[c, i, :, rows],
            soon_ssem.at[c, i], soon_rsem.at[c, i], y_to(i),
        )

    def late_send(c, i):
        rows = pl.ds(i * half, half)
        return remote(
            part.at[c, :, y_next(i), rows], part_in.at[c, i, :, rows],
            late_ssem.at[c, i], late_rsem.at[c, i], y_to(i),
        )

    def cross_send(c):
        return remote(cross.at[c], cross_in.at[c], cross_ssem.at[c], cross_rsem.at[c], z_peer)

    def gz_send(c):
        place = grads.at[c, zh, y]
        return remote(place, place, gz_ssem.at[c], gz_rsem.at[c], z_peer)

    def gz_recv(c):
        place = grads.at[c, 1 - zh, y]
        return remote(place, place, gz_ssem.at[c], gz_rsem.at[c], z_peer)

    def gy_send(c, side, i):
        place = grads.at[c, side, y]
        at = 2 * side + i
        return remote(place, place, gy_ssem.at[c, at], gy_rsem.at[c, at], y_to(i))

    def gy_recv(c, side, i):
        place = grads.at[c, side, y_next(1 - i)]
        at = 2 * side + i
        return remote(place, place, gy_ssem.at[c, at], gy_rsem.at[c, at], y_to(i))

    def relay_send(c, side, i):
        place = grads.at[c, side, y_next(1 - i), pl.ds(i * half, half)]
        at = 2 * side + i
        return remote(place, place, relay_ssem.at[c, at], relay_rsem.at[c, at], y_to(i))

    def relay_recv(c, side, i):
        place = grads.at[c, side, lax.rem(y + 2, Y), pl.ds(i * half, half)]
        at = 2 * side + i
        return remote(place, place, relay_ssem.at[c, at], relay_rsem.at[c, at], y_to(i))

    def core_send(c):
        return remote(
            sums.at[c, 1 - core], core_in.at[c], core_ssem.at[c], core_rsem.at[c], core_peer
        )

    def near_send(c):
        return remote(
            sums.at[c, core, 1 - b0], near_in.at[c], near_ssem.at[c], near_rsem.at[c], near_peer
        )

    def far_send(c):
        return remote(
            sums.at[c, core, b0, 1 - b1], far_in.at[c], far_ssem.at[c], far_rsem.at[c], far_peer
        )

    def store(c):
        cols = pl.ds(pl.multiple_of(c * cw, cw), cw)
        return pltpu.make_async_copy(result.at[c], out.at[:, cols], out_sem.at[c])

    def product(c):
        load_w(c).wait()

        def some(j, carry):
            rows = states[j].reshape(tokens, block_rows)
            part[c, j // Y, lax.rem(j, Y)] = jnp.dot(
                rows, w[c], preferred_element_type=jnp.float32
            ).astype(jnp.bfloat16)
            return carry

        lax.fori_loop(0, 2 * Y, some, 0)
        for i in range(2):
            half_send(c, i).start()
        for i in range(2):
            soon_send(c, i).start()

    def add_half(c):
        for i in range(2):
            half_send(c, i).wait_recv()
            rows = pl.ds(i * half, half)
            part[c, :, y_next(i), rows] = (
                part[c, :, y_next(i), rows].astype(jnp.float32)
                + half_in[c, i].astype(jnp.float32)
            ).astype(jnp.bfloat16)
            late_send(c, i).start()

    def mask_states():
        def some(j, carry):
            rows = states[j].reshape(tokens, block_rows)
            turned = rows.astype(jnp.float32).T
            labels = segments[pl.ds(j, 1), :]
            for e in range(EX):
                masked[j * EX + e] = jnp.where(labels == e, turned, 0.0).astype(jnp.bfloat16)
            return carry

        lax.fori_loop(0, 2 * Y, some, 0)

    def add_up(c):
        for i in range(2):
            soon_send(c, i).wait_recv()
            late_send(c, i).wait_recv()

        def total(side):
            acc = part[c, side, y].astype(jnp.float32)
            for i in range(2):
                acc += part_in[c, i, side].astype(jnp.float32)
            return acc

        cross[c] = total(1 - zh).astype(jnp.bfloat16)
        cross_send(c).start()
        own[c] = total(zh)

    def gradient(c):
        load_cot(c).wait()
        cross_send(c).wait_recv()
        pre = (own[c] + cross_in[c].astype(jnp.float32)) * scale
        sig = jax.nn.sigmoid(pre)
        grads[c, zh, y] = (
            cot[c].astype(jnp.float32) * sig * (1.0 + pre * (1.0 - sig))
        ).astype(jnp.bfloat16)
        gz_send(c).start()
        for i in range(2):
            gy_send(c, zh, i).start()

    def relay(c, side):
        for i in range(2):
            gy_recv(c, side, i).wait_recv()
            relay_send(c, side, i).start()

    def pass_on(c):
        gz_recv(c).wait_recv()
        for i in range(2):
            gy_send(c, 1 - zh, i).start()
        relay(c, zh)

    def relay_far(c):
        relay(c, 1 - zh)

    def fishers(c):
        for side in range(2):
            for i in range(2):
                relay_recv(c, side, i).wait_recv()

        def some(r, carry):
            rows = pl.ds(pl.multiple_of(r * ROWS_AT_ONCE, ROWS_AT_ONCE), ROWS_AT_ONCE)
            acc = jnp.zeros((ROWS_AT_ONCE, cw), jnp.float32)
            for j in range(2 * Y):
                cols = grads[c, j // Y, j % Y]
                for e in range(EX):
                    grad = jnp.dot(
                        masked[j * EX + e, rows, :], cols, preferred_element_type=jnp.float32
                    )
                    acc += grad * grad
            fisher[rows, :] = acc
            return carry

        lax.fori_loop(0, block_rows // ROWS_AT_ONCE, some, 0)
        per = block_rows // 8
        for m in range(8):
            f = fisher[m * per : (m + 1) * per, :]
            at = sums.at[c, m % 2, (m // 2) % 2, m // 4]
            at[0] = (f * w[c, m * per : (m + 1) * per, :].astype(jnp.float32)).astype(jnp.bfloat16)
            at[1] = f.astype(jnp.bfloat16)
        core_send(c).start()

    def add_core(c):
        core_send(c).wait_recv()
        for i in (0, 1):
            side = b0 if i else 1 - b0
            sums[c, core, side] = (
                sums[c, core, side].astype(jnp.float32) + core_in[c, side].astype(jnp.float32)
            ).astype(jnp.bfloat16)
            if i == 0:
                near_send(c).start()

    def add_near(c):
        near_send(c).wait_recv()
        for i in (0, 1):
            side = b1 if i else 1 - b1
            sums[c, core, b0, side] = (
                sums[c, core, b0, side].astype(jnp.float32)
                + near_in[c, side].astype(jnp.float32)
            ).astype(jnp.bfloat16)
            if i == 0:
                far_send(c).start()

    def add_far(c):
        far_send(c).wait_recv()
        both = sums[c, core, b0, b1].astype(jnp.float32) + far_in[c].astype(jnp.float32)
        result[c] = (both[0] / both[1]).astype(jnp.bfloat16)
        store(c).start()

    stages = [
        (product, 0), (add_half, LAG_HALF), (add_up, LAG_SUM), (gradient, LAG_GRAD),
        (pass_on, LAG_PASS), (relay_far, LAG_RELAY),
        (fishers, LAG_FISHER), (add_core, LAG_CORE), (add_near, LAG_NEAR), (add_far, LAG_FAR),
    ]

    def step(t, carry):
        for stage, lag in stages:
            c = t - lag

            @pl.when(jnp.logical_and(c >= 0, c < chunks))
            def _():
                stage(c)

            if stage is product:

                @pl.when(t == 0)
                def _():
                    mask_states()

        return carry

    lax.fori_loop(0, chunks + LAG_FAR, step, 0)

    for b in range(2):
        for q in range(Y):

            @pl.when(jnp.logical_not(to_self(b, q)))
            def _():
                hid_send(b, q).wait_send()

    for side in range(2):
        for d in range(1, Y):
            x_send(side, d).wait_send()

    def finish(c, carry):
        for i in range(2):
            half_send(c, i).wait_send()
            soon_send(c, i).wait_send()
            late_send(c, i).wait_send()
            for side in range(2):
                gy_send(c, side, i).wait_send()
                relay_send(c, side, i).wait_send()
        cross_send(c).wait_send()
        gz_send(c).wait_send()
        core_send(c).wait_send()
        near_send(c).wait_send()
        far_send(c).wait_send()
        store(c).wait()
        return carry

    lax.fori_loop(0, chunks, finish, 0)


def shards(hidden, cotangent, weights, segments):
    tokens, block_rows, columns = hidden.shape[1], weights.shape[1], weights.shape[2]
    cw = CHUNK
    n = columns // cw
    per = block_rows // 8
    bf, f32 = jnp.bfloat16, jnp.float32
    dma = pltpu.SemaphoreType.DMA
    buffers = [
        pltpu.VMEM((n, block_rows, cw), bf),
        pltpu.VMEM((n, tokens, cw), bf),
        pltpu.VMEM((2 * Y, Y, tokens // Y, block_rows), bf),
        pltpu.VMEM((2 * Y * EX, block_rows, tokens), bf),
        pltpu.VMEM((n, 2, Y, tokens, cw), bf),
        pltpu.VMEM((n, 2, 2, tokens // 2, cw), bf),
        pltpu.VMEM((n, 2, 2, tokens, cw), bf),
        pltpu.VMEM((n, tokens, cw), f32),
        pltpu.VMEM((n, tokens, cw), bf),
        pltpu.VMEM((n, tokens, cw), bf),
        pltpu.VMEM((n, 2, Y, tokens, cw), bf),
        pltpu.VMEM((n, 2, 2, 2, 2, per, cw), bf),
        pltpu.VMEM((n, 2, 2, 2, per, cw), bf),
        pltpu.VMEM((n, 2, 2, per, cw), bf),
        pltpu.VMEM((n, 2, per, cw), bf),
        pltpu.VMEM((n, per, cw), bf),
        pltpu.VMEM((block_rows, cw), f32),
    ]
    one, two, four = ([dma((n,) + more)] * 2 for more in ((), (2,), (4,)))
    crossing = [dma((2 * Y,))] * 2 + [dma((2 * (Y - 1),))] * 2
    sems = [dma((2 * n,))] + crossing + [dma((n,))]
    sems += two + two + two + one + one + four + four + one + one + one
    return pl.pallas_call(
        kernel,
        out_shape=jax.ShapeDtypeStruct((per, columns), bf),
        in_specs=[pl.BlockSpec(memory_space=pl.ANY)] * 3
        + [pl.BlockSpec(memory_space=pltpu.VMEM)],
        out_specs=pl.BlockSpec(memory_space=pl.ANY),
        scratch_shapes=buffers + sems,
        compiler_params=pltpu.CompilerParams(
            collective_id=0, has_side_effects=True, vmem_limit_bytes=60 * 2**20
        ),
    )(hidden, cotangent, weights, segments)


def solution(mesh):
    return jax.shard_map(
        shards,
        mesh=mesh,
        in_specs=(P("mp", "dp", "shard"), P("mp", "dp", "shard"), P("mp", "dp", "shard"), P()),
        out_specs=P(("dp", "mp"), "shard"),
        check_vma=False,
    )
```

```python
import math

import jax
import jax.numpy as jnp
from jax import lax
from jax.experimental import pallas as pl
from jax.experimental.pallas import tpu as pltpu
from jax.sharding import PartitionSpec as P

EX = 3
Y = 4
CHUNK = 256
ROWS_AT_ONCE = 64
LAG_HALF, LAG_SUM, LAG_GRAD, LAG_PASS, LAG_RELAY = 1, 2, 4, 6, 7
LAG_FISHER, LAG_CORE, LAG_NEAR, LAG_FAR = 8, 9, 10, 11


def kernel(
    hidden, cotangent, weights, segments, out,
    w, cot, states, masked, part, half_in, part_in, own, cross, cross_in, grads, sums,
    core_in, near_in, far_in, result, fisher,
    load_sem, hid_ssem, hid_rsem, x_ssem, x_rsem, out_sem,
    half_ssem, half_rsem, soon_ssem, soon_rsem, late_ssem, late_rsem, cross_ssem, cross_rsem,
    gz_ssem, gz_rsem, gy_ssem, gy_rsem, relay_ssem, relay_rsem,
    core_ssem, core_rsem, near_ssem, near_rsem, far_ssem, far_rsem,
):
    chunks, block_rows, cw = w.shape
    tokens = cot.shape[1]
    quarter = tokens // Y
    scale = 1.0 / math.sqrt(block_rows * 2 * Y)
    mp, dp, sh = lax.axis_index("mp"), lax.axis_index("dp"), lax.axis_index("shard")
    core, b0, b1 = lax.rem(mp, 2), lax.rem(mp // 2, 2), mp // 4
    zh, y = dp // Y, lax.rem(dp, Y)

    def y_peer(d):
        return {"dp": zh * Y + lax.rem(y + d, Y)}

    def x_peer(d):
        return {"shard": lax.rem(sh + d, Y)}

    z_peer = {"dp": (1 - zh) * Y + y}
    core_peer = {"mp": mp + 1 - 2 * core}
    near_peer = {"mp": mp + 2 - 4 * b0}
    far_peer = {"mp": mp + 4 - 8 * b1}

    def remote(src, dst, ssem, rsem, device):
        return pltpu.make_async_remote_copy(
            src_ref=src,
            dst_ref=dst,
            send_sem=ssem,
            recv_sem=rsem,
            device_id=device,
            device_id_type=pl.DeviceIdType.MESH,
        )

    def load_w(c):
        cols = pl.ds(pl.multiple_of(c * cw, cw), cw)
        return pltpu.make_async_copy(weights.at[0, :, cols], w.at[c], load_sem.at[c])

    def load_cot(c):
        cols = pl.ds(pl.multiple_of(c * cw, cw), cw)
        return pltpu.make_async_copy(
            cotangent.at[0, :, cols], cot.at[c], load_sem.at[chunks + c]
        )

    def start_loads(c, carry):
        load_w(c).start()
        load_cot(c).start()
        return carry

    lax.fori_loop(0, chunks, start_loads, 0)

    barrier = pltpu.get_barrier_semaphore()

    def greet(device):
        pl.semaphore_signal(
            barrier, inc=1, device_id=device, device_id_type=pl.DeviceIdType.MESH
        )

    def from_self(j):
        return jnp.logical_and(sh == dp // 2, dp == j)

    def to_self(b, q):
        return jnp.logical_and(dp == 2 * sh + b, sh == q)

    peers = [y_peer(1), y_peer(3), x_peer(1), x_peer(2), x_peer(3)]
    peers += [z_peer, core_peer, near_peer, far_peer]
    for device in peers:
        greet(device)
    for j in range(2 * Y):

        @pl.when(jnp.logical_not(from_self(j)))
        def _():
            greet({"dp": j, "shard": dp // 2})

    at_home = jnp.where(sh == dp // 2, 1, 0)
    pl.semaphore_wait(barrier, len(peers) + 2 * Y - at_home)

    def hid_send(b, q):
        return remote(
            hidden.at[0, pl.ds(q * quarter, quarter), pl.ds(b * block_rows, block_rows)],
            states.at[dp, q],
            hid_ssem.at[b * Y + q],
            hid_rsem.at[dp],
            {"dp": 2 * sh + b, "shard": q},
        )

    def hid_local(b, q):
        return pltpu.make_async_copy(
            hidden.at[0, pl.ds(q * quarter, quarter), pl.ds(b * block_rows, block_rows)],
            states.at[dp, q],
            hid_ssem.at[b * Y + q],
        )

    def hid_recv(j):
        return remote(
            states.at[j, sh], states.at[j, sh], hid_ssem.at[0], hid_rsem.at[j], {"dp": j, "shard": dp // 2}
        )

    for b in range(2):
        for q in range(Y):

            @pl.when(to_self(b, q))
            def _():
                hid_local(b, q).start()

            @pl.when(jnp.logical_not(to_self(b, q)))
            def _():
                hid_send(b, q).start()

    def x_send(j, d):
        place = states.at[j, sh]
        return remote(place, place, x_ssem.at[d - 1], x_rsem.at[j, d - 1], x_peer(d))

    def x_recv(j, d):
        place = states.at[j, lax.rem(sh - d + Y, Y)]
        return remote(place, place, x_ssem.at[d - 1], x_rsem.at[j, d - 1], x_peer(d))

    def x_forward(j):
        @pl.when(jnp.logical_not(from_self(j)))
        def _():
            hid_recv(j).wait_recv()

        @pl.when(from_self(j))
        def _():
            hid_local(lax.rem(dp, 2), sh).wait()

        for d in range(1, Y):
            x_send(j, d).start()

    for side in (zh, 1 - zh):
        for i in range(Y):
            x_forward(side * Y + i)
    for j in range(2 * Y):
        for d in range(1, Y):
            x_recv(j, d).wait_recv()

    half = tokens // 2

    def y_next(i):
        return lax.rem(y + (1, Y - 1)[i], Y)

    def y_to(i):
        return y_peer((1, Y - 1)[i])

    def half_send(c, i):
        return remote(
            part.at[c, :, lax.rem(y + 2, Y), pl.ds(i * half, half)], half_in.at[c, i],
            half_ssem, half_rsem.at[c, i], y_to(i),
        )

    def soon_send(c, i):
        rows = pl.ds((1 - i) * half, half)
        return remote(
            part.at[c, :, y_next(i), rows], part_in.at[c, i, :, rows],
            soon_ssem, soon_rsem.at[c, i], y_to(i),
        )

    def late_send(c, i):
        rows = pl.ds(i * half, half)
        return remote(
            part.at[c, :, y_next(i), rows], part_in.at[c, i, :, rows],
            late_ssem, late_rsem.at[c, i], y_to(i),
        )

    def cross_send(c):
        return remote(cross.at[c], cross_in.at[c], cross_ssem, cross_rsem.at[c], z_peer)

    def gz_send(c):
        place = grads.at[c, zh, y]
        return remote(place, place, gz_ssem, gz_rsem.at[c], z_peer)

    def gz_recv(c):
        place = grads.at[c, 1 - zh, y]
        return remote(place, place, gz_ssem, gz_rsem.at[c], z_peer)

    def gy_send(c, side, i):
        place = grads.at[c, side, y]
        at = 2 * side + i
        return remote(place, place, gy_ssem, gy_rsem.at[c, at], y_to(i))

    def gy_recv(c, side, i):
        place = grads.at[c, side, y_next(1 - i)]
        at = 2 * side + i
        return remote(place, place, gy_ssem, gy_rsem.at[c, at], y_to(i))

    def relay_send(c, side, i):
        place = grads.at[c, side, y_next(1 - i), pl.ds(i * half, half)]
        at = 2 * side + i
        return remote(place, place, relay_ssem, relay_rsem.at[c, at], y_to(i))

    def relay_recv(c, side, i):
        place = grads.at[c, side, lax.rem(y + 2, Y), pl.ds(i * half, half)]
        at = 2 * side + i
        return remote(place, place, relay_ssem, relay_rsem.at[c, at], y_to(i))

    def core_send(c):
        return remote(
            sums.at[c, 1 - core], core_in.at[c], core_ssem, core_rsem.at[c], core_peer
        )

    def near_send(c):
        return remote(
            sums.at[c, core, 1 - b0], near_in.at[c], near_ssem, near_rsem.at[c], near_peer
        )

    def far_send(c):
        return remote(
            sums.at[c, core, b0, 1 - b1], far_in.at[c], far_ssem, far_rsem.at[c], far_peer
        )

    def store(c):
        cols = pl.ds(pl.multiple_of(c * cw, cw), cw)
        return pltpu.make_async_copy(result.at[c], out.at[:, cols], out_sem.at[c])

    def product(c):
        load_w(c).wait()

        def some(j, carry):
            rows = states[j].reshape(tokens, block_rows)
            part[c, j // Y, lax.rem(j, Y)] = jnp.dot(
                rows, w[c], preferred_element_type=jnp.float32
            ).astype(jnp.bfloat16)
            return carry

        lax.fori_loop(0, 2 * Y, some, 0)
        for i in range(2):
            half_send(c, i).start()
        for i in range(2):
            soon_send(c, i).start()

    def add_half(c):
        for i in range(2):
            half_send(c, i).wait_recv()
            rows = pl.ds(i * half, half)
            part[c, :, y_next(i), rows] = (
                part[c, :, y_next(i), rows].astype(jnp.float32)
                + half_in[c, i].astype(jnp.float32)
            ).astype(jnp.bfloat16)
            late_send(c, i).start()

    def mask_states(first, last):
        def some(j, carry):
            rows = states[j].reshape(tokens, block_rows)
            turned = rows.astype(jnp.float32).T
            labels = segments[pl.ds(j, 1), :]
            for e in range(EX):
                masked[j * EX + e] = jnp.where(labels == e, turned, 0.0).astype(jnp.bfloat16)
            return carry

        lax.fori_loop(first, last, some, 0)

    def add_up(c):
        for i in range(2):
            soon_send(c, i).wait_recv()
            late_send(c, i).wait_recv()

        def total(side):
            acc = part[c, side, y].astype(jnp.float32)
            for i in range(2):
                acc += part_in[c, i, side].astype(jnp.float32)
            return acc

        cross[c] = total(1 - zh).astype(jnp.bfloat16)
        cross_send(c).start()
        own[c] = total(zh)

    def gradient(c):
        load_cot(c).wait()
        cross_send(c).wait_recv()
        pre = (own[c] + cross_in[c].astype(jnp.float32)) * scale
        sig = jax.nn.sigmoid(pre)
        grads[c, zh, y] = (
            cot[c].astype(jnp.float32) * sig * (1.0 + pre * (1.0 - sig))
        ).astype(jnp.bfloat16)
        gz_send(c).start()
        for i in range(2):
            gy_send(c, zh, i).start()

    def relay(c, side):
        for i in range(2):
            gy_recv(c, side, i).wait_recv()
            relay_send(c, side, i).start()

    def pass_on(c):
        gz_recv(c).wait_recv()
        for i in range(2):
            gy_send(c, 1 - zh, i).start()
        relay(c, zh)

    def relay_far(c):
        relay(c, 1 - zh)

    def fishers(c):
        for side in range(2):
            for i in range(2):
                relay_recv(c, side, i).wait_recv()

        def some(r, carry):
            rows = pl.ds(pl.multiple_of(r * ROWS_AT_ONCE, ROWS_AT_ONCE), ROWS_AT_ONCE)
            acc = jnp.zeros((ROWS_AT_ONCE, cw), jnp.float32)
            for j in range(2 * Y):
                cols = grads[c, j // Y, j % Y]
                for e in range(EX):
                    grad = jnp.dot(
                        masked[j * EX + e, rows, :], cols, preferred_element_type=jnp.float32
                    )
                    acc += grad * grad
            fisher[rows, :] = acc
            return carry

        lax.fori_loop(0, block_rows // ROWS_AT_ONCE, some, 0)
        per = block_rows // 8
        for m in range(8):
            f = fisher[m * per : (m + 1) * per, :]
            at = sums.at[c, m % 2, (m // 2) % 2, m // 4]
            at[0] = (f * w[c, m * per : (m + 1) * per, :].astype(jnp.float32)).astype(jnp.bfloat16)
            at[1] = f.astype(jnp.bfloat16)
        core_send(c).start()

    def add_core(c):
        core_send(c).wait_recv()
        for i in (0, 1):
            side = b0 if i else 1 - b0
            sums[c, core, side] = (
                sums[c, core, side].astype(jnp.float32) + core_in[c, side].astype(jnp.float32)
            ).astype(jnp.bfloat16)
            if i == 0:
                near_send(c).start()

    def add_near(c):
        near_send(c).wait_recv()
        for i in (0, 1):
            side = b1 if i else 1 - b1
            sums[c, core, b0, side] = (
                sums[c, core, b0, side].astype(jnp.float32)
                + near_in[c, side].astype(jnp.float32)
            ).astype(jnp.bfloat16)
            if i == 0:
                far_send(c).start()

    def add_far(c):
        far_send(c).wait_recv()
        both = sums[c, core, b0, b1].astype(jnp.float32) + far_in[c].astype(jnp.float32)
        result[c] = (both[0] / both[1]).astype(jnp.bfloat16)
        store(c).start()

    stages = [
        (product, 0), (add_half, LAG_HALF), (add_up, LAG_SUM), (gradient, LAG_GRAD),
        (pass_on, LAG_PASS), (relay_far, LAG_RELAY),
        (fishers, LAG_FISHER), (add_core, LAG_CORE), (add_near, LAG_NEAR), (add_far, LAG_FAR),
    ]

    def step(t, carry):
        for stage, lag in stages:
            c = t - lag

            @pl.when(jnp.logical_and(c >= 0, c < chunks))
            def _():
                stage(c)

        @pl.when(jnp.logical_and(t >= 1, t <= Y))
        def _():
            mask_states(2 * t - 2, 2 * t)

        return carry

    lax.fori_loop(0, chunks + LAG_FAR, step, 0)

    for b in range(2):
        for q in range(Y):

            @pl.when(jnp.logical_not(to_self(b, q)))
            def _():
                hid_send(b, q).wait_send()

    def sent(ref, ssem):
        remote(ref, ref, ssem, cross_rsem.at[0], z_peer).wait_send()

    for i in range(1, Y):
        sent(states.at[:, 0], x_ssem.at[i - 1])
    sent(half_in, half_ssem)
    sent(half_in, soon_ssem)
    sent(half_in, late_ssem)
    sent(cross, cross_ssem)
    sent(cross, gz_ssem)
    sent(part_in, gy_ssem)
    sent(half_in, relay_ssem)
    sent(core_in, core_ssem)
    sent(near_in, near_ssem)
    sent(far_in, far_ssem)

    def finish(c, carry):
        store(c).wait()
        return carry

    lax.fori_loop(0, chunks, finish, 0)


def shards(hidden, cotangent, weights, segments):
    tokens, block_rows, columns = hidden.shape[1], weights.shape[1], weights.shape[2]
    cw = CHUNK
    n = columns // cw
    per = block_rows // 8
    bf, f32 = jnp.bfloat16, jnp.float32
    dma = pltpu.SemaphoreType.DMA
    buffers = [
        pltpu.VMEM((n, block_rows, cw), bf),
        pltpu.VMEM((n, tokens, cw), bf),
        pltpu.VMEM((2 * Y, Y, tokens // Y, block_rows), bf),
        pltpu.VMEM((2 * Y * EX, block_rows, tokens), bf),
        pltpu.VMEM((n, 2, Y, tokens, cw), bf),
        pltpu.VMEM((n, 2, 2, tokens // 2, cw), bf),
        pltpu.VMEM((n, 2, 2, tokens, cw), bf),
        pltpu.VMEM((n, tokens, cw), f32),
        pltpu.VMEM((n, tokens, cw), bf),
        pltpu.VMEM((n, tokens, cw), bf),
        pltpu.VMEM((n, 2, Y, tokens, cw), bf),
        pltpu.VMEM((n, 2, 2, 2, 2, per, cw), bf),
        pltpu.VMEM((n, 2, 2, 2, per, cw), bf),
        pltpu.VMEM((n, 2, 2, per, cw), bf),
        pltpu.VMEM((n, 2, per, cw), bf),
        pltpu.VMEM((n, per, cw), bf),
        pltpu.VMEM((block_rows, cw), f32),
    ]
    one, two, four = ([dma, dma((n,) + more)] for more in ((), (2,), (4,)))
    crossing = [dma((2 * Y,))] * 2 + [dma((Y - 1,)), dma((2 * Y, Y - 1))]
    sems = [dma((2 * n,))] + crossing + [dma((n,))]
    sems += two + two + two + one + one + four + four + one + one + one
    return pl.pallas_call(
        kernel,
        out_shape=jax.ShapeDtypeStruct((per, columns), bf),
        in_specs=[pl.BlockSpec(memory_space=pl.ANY)] * 3
        + [pl.BlockSpec(memory_space=pltpu.VMEM)],
        out_specs=pl.BlockSpec(memory_space=pl.ANY),
        scratch_shapes=buffers + sems,
        compiler_params=pltpu.CompilerParams(
            collective_id=0, has_side_effects=True, vmem_limit_bytes=60 * 2**20
        ),
    )(hidden, cotangent, weights, segments)


def solution(mesh):
    return jax.shard_map(
        shards,
        mesh=mesh,
        in_specs=(P("mp", "dp", "shard"), P("mp", "dp", "shard"), P("mp", "dp", "shard"), P()),
        out_specs=P(("dp", "mp"), "shard"),
        check_vma=False,
    )
```

```python
import math

import jax
import jax.numpy as jnp
from jax import lax
from jax.experimental import pallas as pl
from jax.experimental.pallas import tpu as pltpu
from jax.sharding import PartitionSpec as P

EX = 3
Y = 4
CHUNK = 256
ROWS_AT_ONCE = 64
LAG_HALF, LAG_SUM, LAG_GRAD, LAG_PASS, LAG_RELAY = 1, 2, 4, 6, 7
LAG_FISHER, LAG_CORE, LAG_NEAR, LAG_FAR = 8, 9, 10, 11


def kernel(
    hidden, cotangent, weights, segments, out,
    w, cot, states, masked, part, half_in, part_in, own, cross, cross_in, grads, sums,
    core_in, near_in, far_in, result, fisher,
    load_sem, cot_sem, hid_ssem, hid_rsem, x_ssem, x_rsem, out_sem,
    half_ssem, half_rsem, part_ssem, part_rsem, cross_ssem, cross_rsem,
    gz_ssem, gz_rsem, gy_ssem, gy_rsem, relay_ssem, relay_rsem,
    core_ssem, core_rsem, near_ssem, near_rsem, far_ssem, far_rsem,
):
    chunks, block_rows, cw = w.shape
    tokens = cot.shape[0]
    quarter = tokens // Y
    scale = 1.0 / math.sqrt(block_rows * 2 * Y)
    mp, dp, sh = lax.axis_index("mp"), lax.axis_index("dp"), lax.axis_index("shard")
    core, b0, b1 = lax.rem(mp, 2), lax.rem(mp // 2, 2), mp // 4
    zh, y = dp // Y, lax.rem(dp, Y)

    def y_peer(d):
        return {"dp": zh * Y + lax.rem(y + d, Y)}

    def x_peer(d):
        return {"shard": lax.rem(sh + d, Y)}

    z_peer = {"dp": (1 - zh) * Y + y}
    core_peer = {"mp": mp + 1 - 2 * core}
    near_peer = {"mp": mp + 2 - 4 * b0}
    far_peer = {"mp": mp + 4 - 8 * b1}

    def remote(src, dst, ssem, rsem, device):
        return pltpu.make_async_remote_copy(
            src_ref=src,
            dst_ref=dst,
            send_sem=ssem,
            recv_sem=rsem,
            device_id=device,
            device_id_type=pl.DeviceIdType.MESH,
        )

    def load_w(c):
        cols = pl.ds(pl.multiple_of(c * cw, cw), cw)
        return pltpu.make_async_copy(weights.at[0, :, cols], w.at[c], load_sem.at[c])

    load_cot = pltpu.make_async_copy(cotangent.at[0], cot, cot_sem)

    def start_loads(c, carry):
        load_w(c).start()
        return carry

    load_cot.start()
    lax.fori_loop(0, chunks, start_loads, 0)

    barrier = pltpu.get_barrier_semaphore()

    def greet(device):
        pl.semaphore_signal(
            barrier, inc=1, device_id=device, device_id_type=pl.DeviceIdType.MESH
        )

    def from_self(j):
        return jnp.logical_and(sh == dp // 2, dp == j)

    def to_self(b, q):
        return jnp.logical_and(dp == 2 * sh + b, sh == q)

    peers = [y_peer(1), y_peer(3), x_peer(1), x_peer(2), x_peer(3)]
    peers += [z_peer, core_peer, near_peer, far_peer]
    for device in peers:
        greet(device)
    for j in range(2 * Y):

        @pl.when(jnp.logical_not(from_self(j)))
        def _():
            greet({"dp": j, "shard": dp // 2})

    at_home = jnp.where(sh == dp // 2, 1, 0)
    pl.semaphore_wait(barrier, len(peers) + 2 * Y - at_home)

    def hid_send(b, q):
        return remote(
            hidden.at[0, pl.ds(q * quarter, quarter), pl.ds(b * block_rows, block_rows)],
            states.at[dp, q],
            hid_ssem.at[b * Y + q],
            hid_rsem.at[dp],
            {"dp": 2 * sh + b, "shard": q},
        )

    def hid_local(b, q):
        return pltpu.make_async_copy(
            hidden.at[0, pl.ds(q * quarter, quarter), pl.ds(b * block_rows, block_rows)],
            states.at[dp, q],
            hid_ssem.at[b * Y + q],
        )

    def hid_recv(j):
        return remote(
            states.at[j, sh], states.at[j, sh], hid_ssem.at[0], hid_rsem.at[j], {"dp": j, "shard": dp // 2}
        )

    for b in range(2):
        for q in range(Y):

            @pl.when(to_self(b, q))
            def _():
                hid_local(b, q).start()

            @pl.when(jnp.logical_not(to_self(b, q)))
            def _():
                hid_send(b, q).start()

    def x_send(j, d):
        place = states.at[j, sh]
        return remote(place, place, x_ssem.at[d - 1], x_rsem, x_peer(d))

    def x_forward(j):
        @pl.when(jnp.logical_not(from_self(j)))
        def _():
            hid_recv(j).wait_recv()

        @pl.when(from_self(j))
        def _():
            hid_local(lax.rem(dp, 2), sh).wait()

        for d in range(1, Y):
            x_send(j, d).start()

    for side in (zh, 1 - zh):
        for i in range(Y):
            x_forward(side * Y + i)
    others = states.at[:, pl.ds(0, Y - 1)]
    remote(others, others, x_ssem.at[0], x_rsem, x_peer(1)).wait_recv()

    half = tokens // 2

    def y_next(i):
        return lax.rem(y + (1, Y - 1)[i], Y)

    def y_to(i):
        return y_peer((1, Y - 1)[i])

    def half_send(c, i):
        return remote(
            part.at[c, :, lax.rem(y + 2, Y), pl.ds(i * half, half)], half_in.at[c, i],
            half_ssem, half_rsem.at[c], y_to(i),
        )

    def soon_send(c, i):
        rows = pl.ds((1 - i) * half, half)
        return remote(
            part.at[c, :, y_next(i), rows], part_in.at[c, i, :, rows],
            part_ssem, part_rsem.at[c], y_to(i),
        )

    def late_send(c, i):
        rows = pl.ds(i * half, half)
        return remote(
            part.at[c, :, y_next(i), rows], part_in.at[c, i, :, rows],
            part_ssem, part_rsem.at[c], y_to(i),
        )

    def cross_send(c):
        return remote(cross.at[c], cross_in.at[c], cross_ssem, cross_rsem.at[c], z_peer)

    def gz_send(c):
        place = grads.at[c, zh, y]
        return remote(place, place, gz_ssem, gz_rsem.at[c], z_peer)

    def gz_recv(c):
        place = grads.at[c, 1 - zh, y]
        return remote(place, place, gz_ssem, gz_rsem.at[c], z_peer)

    def gy_send(c, side, i):
        place = grads.at[c, side, y]
        return remote(place, place, gy_ssem, gy_rsem.at[c, side], y_to(i))

    def arrived(ref, rsem):
        remote(ref, ref, cross_ssem, rsem, z_peer).wait_recv()

    def relay_send(c, side, i):
        place = grads.at[c, side, y_next(1 - i), pl.ds(i * half, half)]
        return remote(place, place, relay_ssem, relay_rsem.at[c], y_to(i))

    def core_send(c):
        return remote(
            sums.at[c, 1 - core], core_in.at[c], core_ssem, core_rsem.at[c], core_peer
        )

    def near_send(c):
        return remote(
            sums.at[c, core, 1 - b0], near_in.at[c], near_ssem, near_rsem.at[c], near_peer
        )

    def far_send(c):
        return remote(
            sums.at[c, core, b0, 1 - b1], far_in.at[c], far_ssem, far_rsem.at[c], far_peer
        )

    def store(c):
        cols = pl.ds(pl.multiple_of(c * cw, cw), cw)
        return pltpu.make_async_copy(result.at[c], out.at[:, cols], out_sem)

    def product(c):
        load_w(c).wait()

        def some(j, carry):
            rows = states[j].reshape(tokens, block_rows)
            part[c, j // Y, lax.rem(j, Y)] = jnp.dot(
                rows, w[c], preferred_element_type=jnp.float32
            ).astype(jnp.bfloat16)
            return carry

        lax.fori_loop(0, 2 * Y, some, 0)
        for i in range(2):
            half_send(c, i).start()
        for i in range(2):
            soon_send(c, i).start()

    def add_half(c):
        arrived(half_in.at[c], half_rsem.at[c])
        for i in range(2):
            rows = pl.ds(i * half, half)
            part[c, :, y_next(i), rows] = (
                part[c, :, y_next(i), rows].astype(jnp.float32)
                + half_in[c, i].astype(jnp.float32)
            ).astype(jnp.bfloat16)
            late_send(c, i).start()

    def mask_states(first, last):
        def some(j, carry):
            rows = states[j].reshape(tokens, block_rows)
            turned = rows.astype(jnp.float32).T
            labels = segments[pl.ds(j, 1), :]
            for e in range(EX):
                masked[j * EX + e] = jnp.where(labels == e, turned, 0.0).astype(jnp.bfloat16)
            return carry

        lax.fori_loop(first, last, some, 0)

    def add_up(c):
        arrived(part_in.at[c], part_rsem.at[c])

        def total(side):
            acc = part[c, side, y].astype(jnp.float32)
            for i in range(2):
                acc += part_in[c, i, side].astype(jnp.float32)
            return acc

        cross[c] = total(1 - zh).astype(jnp.bfloat16)
        cross_send(c).start()
        own[c] = total(zh)

    def gradient(c):
        cross_send(c).wait_recv()
        pre = (own[c] + cross_in[c].astype(jnp.float32)) * scale
        sig = jax.nn.sigmoid(pre)
        grads[c, zh, y] = (
            cot[:, pl.ds(pl.multiple_of(c * cw, cw), cw)].astype(jnp.float32) * sig * (1.0 + pre * (1.0 - sig))
        ).astype(jnp.bfloat16)
        gz_send(c).start()
        for i in range(2):
            gy_send(c, zh, i).start()

    def relay(c, side):
        arrived(grads.at[c, side, pl.ds(0, 2)], gy_rsem.at[c, side])
        for i in range(2):
            relay_send(c, side, i).start()

    def pass_on(c):
        gz_recv(c).wait_recv()
        for i in range(2):
            gy_send(c, 1 - zh, i).start()
        relay(c, zh)

    def relay_far(c):
        relay(c, 1 - zh)

    def fishers(c):
        arrived(grads.at[c, 0, pl.ds(0, 2)], relay_rsem.at[c])

        def some(r, carry):
            rows = pl.ds(pl.multiple_of(r * ROWS_AT_ONCE, ROWS_AT_ONCE), ROWS_AT_ONCE)
            acc = jnp.zeros((ROWS_AT_ONCE, cw), jnp.float32)
            for j in range(2 * Y):
                cols = grads[c, j // Y, j % Y]
                for e in range(EX):
                    grad = jnp.dot(
                        masked[j * EX + e, rows, :], cols, preferred_element_type=jnp.float32
                    )
                    acc += grad * grad
            fisher[rows, :] = acc
            return carry

        lax.fori_loop(0, block_rows // ROWS_AT_ONCE, some, 0)
        per = block_rows // 8
        for m in range(8):
            f = fisher[m * per : (m + 1) * per, :]
            at = sums.at[c, m % 2, (m // 2) % 2, m // 4]
            at[0] = (f * w[c, m * per : (m + 1) * per, :].astype(jnp.float32)).astype(jnp.bfloat16)
            at[1] = f.astype(jnp.bfloat16)
        core_send(c).start()

    def add_core(c):
        core_send(c).wait_recv()
        for i in (0, 1):
            side = b0 if i else 1 - b0
            sums[c, core, side] = (
                sums[c, core, side].astype(jnp.float32) + core_in[c, side].astype(jnp.float32)
            ).astype(jnp.bfloat16)
            if i == 0:
                near_send(c).start()

    def add_near(c):
        near_send(c).wait_recv()
        for i in (0, 1):
            side = b1 if i else 1 - b1
            sums[c, core, b0, side] = (
                sums[c, core, b0, side].astype(jnp.float32)
                + near_in[c, side].astype(jnp.float32)
            ).astype(jnp.bfloat16)
            if i == 0:
                far_send(c).start()

    def add_far(c):
        far_send(c).wait_recv()
        both = sums[c, core, b0, b1].astype(jnp.float32) + far_in[c].astype(jnp.float32)
        result[c] = (both[0] / both[1]).astype(jnp.bfloat16)
        store(c).start()

    stages = [
        (product, 0), (add_half, LAG_HALF), (add_up, LAG_SUM), (gradient, LAG_GRAD),
        (pass_on, LAG_PASS), (relay_far, LAG_RELAY),
        (fishers, LAG_FISHER), (add_core, LAG_CORE), (add_near, LAG_NEAR), (add_far, LAG_FAR),
    ]

    def step(t, carry):
        for stage, lag in stages:
            c = t - lag

            @pl.when(jnp.logical_and(c >= 0, c < chunks))
            def _():
                stage(c)

        @pl.when(jnp.logical_and(t >= 1, t <= Y))
        def _():
            mask_states(2 * t - 2, 2 * t)

        return carry

    load_cot.wait()
    lax.fori_loop(0, chunks + LAG_FAR, step, 0)

    for b in range(2):
        for q in range(Y):

            @pl.when(jnp.logical_not(to_self(b, q)))
            def _():
                hid_send(b, q).wait_send()

    def sent(ref, ssem):
        remote(ref, ref, ssem, cross_rsem.at[0], z_peer).wait_send()

    for i in range(1, Y):
        sent(states.at[:, 0], x_ssem.at[i - 1])
    sent(half_in, half_ssem)
    sent(part_in, part_ssem)
    sent(cross, cross_ssem)
    sent(cross, gz_ssem)
    sent(part_in, gy_ssem)
    sent(half_in, relay_ssem)
    sent(core_in, core_ssem)
    sent(near_in, near_ssem)
    sent(far_in, far_ssem)

    pltpu.make_async_copy(out, out, out_sem).wait()


def shards(hidden, cotangent, weights, segments):
    tokens, block_rows, columns = hidden.shape[1], weights.shape[1], weights.shape[2]
    cw = CHUNK
    n = columns // cw
    per = block_rows // 8
    bf, f32 = jnp.bfloat16, jnp.float32
    dma = pltpu.SemaphoreType.DMA
    buffers = [
        pltpu.VMEM((n, block_rows, cw), bf),
        pltpu.VMEM((tokens, columns), bf),
        pltpu.VMEM((2 * Y, Y, tokens // Y, block_rows), bf),
        pltpu.VMEM((2 * Y * EX, block_rows, tokens), bf),
        pltpu.VMEM((n, 2, Y, tokens, cw), bf),
        pltpu.VMEM((n, 2, 2, tokens // 2, cw), bf),
        pltpu.VMEM((n, 2, 2, tokens, cw), bf),
        pltpu.VMEM((n, tokens, cw), f32),
        pltpu.VMEM((n, tokens, cw), bf),
        pltpu.VMEM((n, tokens, cw), bf),
        pltpu.VMEM((n, 2, Y, tokens, cw), bf),
        pltpu.VMEM((n, 2, 2, 2, 2, per, cw), bf),
        pltpu.VMEM((n, 2, 2, 2, per, cw), bf),
        pltpu.VMEM((n, 2, 2, per, cw), bf),
        pltpu.VMEM((n, 2, per, cw), bf),
        pltpu.VMEM((n, per, cw), bf),
        pltpu.VMEM((block_rows, cw), f32),
    ]
    one, two = [dma, dma((n,))], [dma, dma((n, 2))]
    crossing = [dma((2 * Y,))] * 2 + [dma((Y - 1,)), dma]
    sems = [dma((n,)), dma] + crossing + [dma]
    sems += one + one + one + one + two + one + one + one + one
    return pl.pallas_call(
        kernel,
        out_shape=jax.ShapeDtypeStruct((per, columns), bf),
        in_specs=[pl.BlockSpec(memory_space=pl.ANY)] * 3
        + [pl.BlockSpec(memory_space=pltpu.VMEM)],
        out_specs=pl.BlockSpec(memory_space=pl.ANY),
        scratch_shapes=buffers + sems,
        compiler_params=pltpu.CompilerParams(
            collective_id=0, has_side_effects=True, vmem_limit_bytes=60 * 2**20
        ),
    )(hidden, cotangent, weights, segments)


def solution(mesh):
    return jax.shard_map(
        shards,
        mesh=mesh,
        in_specs=(P("mp", "dp", "shard"), P("mp", "dp", "shard"), P("mp", "dp", "shard"), P()),
        out_specs=P(("dp", "mp"), "shard"),
        check_vma=False,
    )
```

```python
import math

import jax
import jax.numpy as jnp
from jax import lax
from jax.experimental import pallas as pl
from jax.experimental.pallas import tpu as pltpu
from jax.sharding import PartitionSpec as P

EX = 3
Y = 4
CHUNK = 256
DIRECT = 4
ROWS_AT_ONCE = 64
LAG_HALF, LAG_SUM, LAG_GRAD, LAG_PASS, LAG_RELAY = 1, 2, 4, 6, 7
LAG_FISHER, LAG_CORE, LAG_NEAR, LAG_FAR = 8, 9, 11, 12


def kernel(
    hidden, cotangent, weights, segments, out,
    w, cot, states, masked, part, half_in, part_in, own, cross, cross_in, grads, sums,
    core_in, near_in, far_in, result, fisher,
    load_sem, cot_sem, hid_ssem, hid_rsem, x_ssem, x_rsem, out_sem,
    half_ssem, half_rsem, part_ssem, part_rsem, cross_ssem, cross_rsem,
    gz_ssem, gz_rsem, gy_ssem, gy_rsem, relay_ssem, relay_rsem,
    core_ssem, core_rsem, near_ssem, near_rsem, far_ssem, far_rsem,
):
    chunks, block_rows, cw = w.shape
    tokens = cot.shape[0]
    quarter = tokens // Y
    relayed = chunks - DIRECT
    scale = 1.0 / math.sqrt(block_rows * 2 * Y)
    mp, dp, sh = lax.axis_index("mp"), lax.axis_index("dp"), lax.axis_index("shard")
    core, b0, b1 = lax.rem(mp, 2), lax.rem(mp // 2, 2), mp // 4
    zh, y = dp // Y, lax.rem(dp, Y)

    def y_peer(d):
        return {"dp": zh * Y + lax.rem(y + d, Y)}

    def x_peer(d):
        return {"shard": lax.rem(sh + d, Y)}

    z_peer = {"dp": (1 - zh) * Y + y}
    core_peer = {"mp": mp + 1 - 2 * core}
    near_peer = {"mp": mp + 2 - 4 * b0}
    far_peer = {"mp": mp + 4 - 8 * b1}

    def remote(src, dst, ssem, rsem, device):
        return pltpu.make_async_remote_copy(
            src_ref=src,
            dst_ref=dst,
            send_sem=ssem,
            recv_sem=rsem,
            device_id=device,
            device_id_type=pl.DeviceIdType.MESH,
        )

    def load_w(c):
        cols = pl.ds(pl.multiple_of(c * cw, cw), cw)
        return pltpu.make_async_copy(weights.at[0, :, cols], w.at[c], load_sem.at[c])

    load_cot = pltpu.make_async_copy(cotangent.at[0], cot, cot_sem)

    def start_loads(c, carry):
        load_w(c).start()
        return carry

    load_cot.start()
    lax.fori_loop(0, chunks, start_loads, 0)

    barrier = pltpu.get_barrier_semaphore()

    def greet(device):
        pl.semaphore_signal(
            barrier, inc=1, device_id=device, device_id_type=pl.DeviceIdType.MESH
        )

    def from_self(j):
        return jnp.logical_and(sh == dp // 2, dp == j)

    def to_self(b, q):
        return jnp.logical_and(dp == 2 * sh + b, sh == q)

    peers = [y_peer(1), y_peer(2), y_peer(3), x_peer(1), x_peer(2), x_peer(3)]
    peers += [z_peer, core_peer, near_peer, far_peer]
    for device in peers:
        greet(device)
    for j in range(2 * Y):

        @pl.when(jnp.logical_not(from_self(j)))
        def _():
            greet({"dp": j, "shard": dp // 2})

    at_home = jnp.where(sh == dp // 2, 1, 0)
    pl.semaphore_wait(barrier, len(peers) + 2 * Y - at_home)

    def hid_send(b, q):
        return remote(
            hidden.at[0, pl.ds(q * quarter, quarter), pl.ds(b * block_rows, block_rows)],
            states.at[dp, q],
            hid_ssem.at[b * Y + q],
            hid_rsem.at[dp],
            {"dp": 2 * sh + b, "shard": q},
        )

    def hid_local(b, q):
        return pltpu.make_async_copy(
            hidden.at[0, pl.ds(q * quarter, quarter), pl.ds(b * block_rows, block_rows)],
            states.at[dp, q],
            hid_ssem.at[b * Y + q],
        )

    def hid_recv(j):
        return remote(
            states.at[j, sh], states.at[j, sh], hid_ssem.at[0], hid_rsem.at[j], {"dp": j, "shard": dp // 2}
        )

    for b in range(2):
        for q in range(Y):

            @pl.when(to_self(b, q))
            def _():
                hid_local(b, q).start()

            @pl.when(jnp.logical_not(to_self(b, q)))
            def _():
                hid_send(b, q).start()

    def x_send(j, d):
        place = states.at[j, sh]
        return remote(place, place, x_ssem.at[d - 1], x_rsem, x_peer(d))

    def x_forward(j):
        @pl.when(jnp.logical_not(from_self(j)))
        def _():
            hid_recv(j).wait_recv()

        @pl.when(from_self(j))
        def _():
            hid_local(lax.rem(dp, 2), sh).wait()

        for d in range(1, Y):
            x_send(j, d).start()

    for side in (zh, 1 - zh):
        for i in range(Y):
            x_forward(side * Y + i)
    others = states.at[:, pl.ds(0, Y - 1)]
    remote(others, others, x_ssem.at[0], x_rsem, x_peer(1)).wait_recv()

    half = tokens // 2

    def y_next(i):
        return lax.rem(y + (1, Y - 1)[i], Y)

    def y_to(i):
        return y_peer((1, Y - 1)[i])

    def half_send(c, i):
        return remote(
            part.at[c, :, lax.rem(y + 2, Y), pl.ds(i * half, half)], half_in.at[c, i],
            half_ssem, half_rsem.at[c], y_to(i),
        )

    def soon_send(c, i):
        rows = pl.ds((1 - i) * half, half)
        return remote(
            part.at[c, :, y_next(i), rows], part_in.at[c, i, :, rows],
            part_ssem, part_rsem.at[c], y_to(i),
        )

    def late_send(c, i):
        rows = pl.ds(i * half, half)
        return remote(
            part.at[c, :, y_next(i), rows], part_in.at[c, i, :, rows],
            part_ssem, part_rsem.at[c], y_to(i),
        )

    def cross_send(c):
        return remote(cross.at[c], cross_in.at[c], cross_ssem, cross_rsem.at[c], z_peer)

    def gz_send(c):
        place = grads.at[c, zh, y]
        return remote(place, place, gz_ssem, gz_rsem.at[c], z_peer)

    def gz_recv(c):
        place = grads.at[c, 1 - zh, y]
        return remote(place, place, gz_ssem, gz_rsem.at[c], z_peer)

    def gy_send(c, side, i):
        place = grads.at[c, side, y]
        return remote(place, place, gy_ssem, gy_rsem.at[c, side], y_to(i))

    def arrived(ref, rsem):
        remote(ref, ref, cross_ssem, rsem, z_peer).wait_recv()

    def relay_send(c, side, i):
        place = grads.at[c, side, y_next(1 - i), pl.ds(i * half, half)]
        return remote(place, place, relay_ssem, relay_rsem.at[c], y_to(i))

    def direct_send(c, side, i):
        place = grads.at[c, side, y, pl.ds(i * half, half)]
        return remote(place, place, relay_ssem, relay_rsem.at[c], y_peer(2))

    def spread(c, side):
        for i in range(2):
            gy_send(c, side, i).start()

        @pl.when(c >= relayed)
        def _():
            for i in range(2):
                direct_send(c, side, i).start()

    def core_send(c):
        return remote(
            sums.at[c, 1 - core], core_in.at[c], core_ssem, core_rsem.at[c], core_peer
        )

    def near_send(c):
        return remote(
            sums.at[c, core, 1 - b0], near_in.at[c], near_ssem, near_rsem.at[c], near_peer
        )

    def far_send(c):
        return remote(
            sums.at[c, core, b0, 1 - b1], far_in.at[c], far_ssem, far_rsem.at[c], far_peer
        )

    def store(c):
        cols = pl.ds(pl.multiple_of(c * cw, cw), cw)
        return pltpu.make_async_copy(result.at[c], out.at[:, cols], out_sem)

    def product(c):
        load_w(c).wait()

        def some(j, carry):
            rows = states[j].reshape(tokens, block_rows)
            part[c, j // Y, lax.rem(j, Y)] = jnp.dot(
                rows, w[c], preferred_element_type=jnp.float32
            ).astype(jnp.bfloat16)
            return carry

        lax.fori_loop(0, 2 * Y, some, 0)
        for i in range(2):
            half_send(c, i).start()
        for i in range(2):
            soon_send(c, i).start()

    def add_half(c):
        arrived(half_in.at[c], half_rsem.at[c])
        for i in range(2):
            rows = pl.ds(i * half, half)
            part[c, :, y_next(i), rows] = (
                part[c, :, y_next(i), rows].astype(jnp.float32)
                + half_in[c, i].astype(jnp.float32)
            ).astype(jnp.bfloat16)
            late_send(c, i).start()

    def mask_states(first, last):
        def some(j, carry):
            rows = states[j].reshape(tokens, block_rows)
            turned = rows.astype(jnp.float32).T
            labels = segments[pl.ds(j, 1), :]
            for e in range(EX):
                masked[j * EX + e] = jnp.where(labels == e, turned, 0.0).astype(jnp.bfloat16)
            return carry

        lax.fori_loop(first, last, some, 0)

    def add_up(c):
        arrived(part_in.at[c], part_rsem.at[c])

        def total(side):
            acc = part[c, side, y].astype(jnp.float32)
            for i in range(2):
                acc += part_in[c, i, side].astype(jnp.float32)
            return acc

        cross[c] = total(1 - zh).astype(jnp.bfloat16)
        cross_send(c).start()
        own[c] = total(zh)

    def gradient(c):
        cross_send(c).wait_recv()
        pre = (own[c] + cross_in[c].astype(jnp.float32)) * scale
        sig = jax.nn.sigmoid(pre)
        grads[c, zh, y] = (
            cot[:, pl.ds(pl.multiple_of(c * cw, cw), cw)].astype(jnp.float32) * sig * (1.0 + pre * (1.0 - sig))
        ).astype(jnp.bfloat16)
        gz_send(c).start()
        spread(c, zh)

    def relay(c, side):
        arrived(grads.at[c, side, pl.ds(0, 2)], gy_rsem.at[c, side])

        @pl.when(c < relayed)
        def _():
            for i in range(2):
                relay_send(c, side, i).start()

    def pass_on(c):
        gz_recv(c).wait_recv()
        spread(c, 1 - zh)
        relay(c, zh)

    def relay_far(c):
        relay(c, 1 - zh)

    def fishers(c):
        arrived(grads.at[c, 0, pl.ds(0, 2)], relay_rsem.at[c])

        def some(r, carry):
            rows = pl.ds(pl.multiple_of(r * ROWS_AT_ONCE, ROWS_AT_ONCE), ROWS_AT_ONCE)
            acc = jnp.zeros((ROWS_AT_ONCE, cw), jnp.float32)
            for j in range(2 * Y):
                cols = grads[c, j // Y, j % Y]
                for e in range(EX):
                    grad = jnp.dot(
                        masked[j * EX + e, rows, :], cols, preferred_element_type=jnp.float32
                    )
                    acc += grad * grad
            fisher[rows, :] = acc
            return carry

        lax.fori_loop(0, block_rows // ROWS_AT_ONCE, some, 0)
        per = block_rows // 8
        for m in range(8):
            f = fisher[m * per : (m + 1) * per, :]
            at = sums.at[c, m % 2, (m // 2) % 2, m // 4]
            at[0] = (f * w[c, m * per : (m + 1) * per, :].astype(jnp.float32)).astype(jnp.bfloat16)
            at[1] = f.astype(jnp.bfloat16)
        core_send(c).start()

    def add_core(c):
        core_send(c).wait_recv()
        for i in (0, 1):
            side = b0 if i else 1 - b0
            sums[c, core, side] = (
                sums[c, core, side].astype(jnp.float32) + core_in[c, side].astype(jnp.float32)
            ).astype(jnp.bfloat16)
            if i == 0:
                near_send(c).start()

    def add_near(c):
        near_send(c).wait_recv()
        for i in (0, 1):
            side = b1 if i else 1 - b1
            sums[c, core, b0, side] = (
                sums[c, core, b0, side].astype(jnp.float32)
                + near_in[c, side].astype(jnp.float32)
            ).astype(jnp.bfloat16)
            if i == 0:
                far_send(c).start()

    def add_far(c):
        far_send(c).wait_recv()
        both = sums[c, core, b0, b1].astype(jnp.float32) + far_in[c].astype(jnp.float32)
        result[c] = (both[0] / both[1]).astype(jnp.bfloat16)
        store(c).start()

    stages = [
        (product, 0), (add_half, LAG_HALF), (add_up, LAG_SUM), (gradient, LAG_GRAD),
        (pass_on, LAG_PASS), (relay_far, LAG_RELAY),
        (fishers, LAG_FISHER), (add_core, LAG_CORE), (add_near, LAG_NEAR), (add_far, LAG_FAR),
    ]

    def step(t, carry):
        for stage, lag in stages:
            if lag < LAG_FISHER:
                c = t - lag

                @pl.when(jnp.logical_and(c >= 0, c < chunks))
                def _():
                    stage(c)

            else:

                def run(u, carry):
                    c = t - lag + u
                    runs = jnp.logical_and(u == 0, jnp.logical_and(c >= 0, c < relayed))
                    direct = jnp.logical_and(u == 1, jnp.logical_and(c >= relayed, c < chunks))

                    @pl.when(jnp.logical_or(runs, direct))
                    def _():
                        stage(c)

                    return carry

                lax.fori_loop(0, 2, run, 0)

        @pl.when(jnp.logical_and(t >= 1, t <= Y))
        def _():
            mask_states(2 * t - 2, 2 * t)

        return carry

    load_cot.wait()
    lax.fori_loop(0, chunks + LAG_FAR - 1, step, 0)

    for b in range(2):
        for q in range(Y):

            @pl.when(jnp.logical_not(to_self(b, q)))
            def _():
                hid_send(b, q).wait_send()

    def sent(ref, ssem):
        remote(ref, ref, ssem, cross_rsem.at[0], z_peer).wait_send()

    for i in range(1, Y):
        sent(states.at[:, 0], x_ssem.at[i - 1])
    sent(half_in, half_ssem)
    sent(part_in, part_ssem)
    sent(cross, cross_ssem)
    sent(cross, gz_ssem)
    sent(part_in, gy_ssem)
    sent(half_in, relay_ssem)
    sent(core_in, core_ssem)
    sent(near_in, near_ssem)
    sent(far_in, far_ssem)

    pltpu.make_async_copy(out, out, out_sem).wait()


def shards(hidden, cotangent, weights, segments):
    tokens, block_rows, columns = hidden.shape[1], weights.shape[1], weights.shape[2]
    cw = CHUNK
    n = columns // cw
    per = block_rows // 8
    bf, f32 = jnp.bfloat16, jnp.float32
    dma = pltpu.SemaphoreType.DMA
    buffers = [
        pltpu.VMEM((n, block_rows, cw), bf),
        pltpu.VMEM((tokens, columns), bf),
        pltpu.VMEM((2 * Y, Y, tokens // Y, block_rows), bf),
        pltpu.VMEM((2 * Y * EX, block_rows, tokens), bf),
        pltpu.VMEM((n, 2, Y, tokens, cw), bf),
        pltpu.VMEM((n, 2, 2, tokens // 2, cw), bf),
        pltpu.VMEM((n, 2, 2, tokens, cw), bf),
        pltpu.VMEM((n, tokens, cw), f32),
        pltpu.VMEM((n, tokens, cw), bf),
        pltpu.VMEM((n, tokens, cw), bf),
        pltpu.VMEM((n, 2, Y, tokens, cw), bf),
        pltpu.VMEM((n, 2, 2, 2, 2, per, cw), bf),
        pltpu.VMEM((n, 2, 2, 2, per, cw), bf),
        pltpu.VMEM((n, 2, 2, per, cw), bf),
        pltpu.VMEM((n, 2, per, cw), bf),
        pltpu.VMEM((n, per, cw), bf),
        pltpu.VMEM((block_rows, cw), f32),
    ]
    one, two = [dma, dma((n,))], [dma, dma((n, 2))]
    crossing = [dma((2 * Y,))] * 2 + [dma((Y - 1,)), dma]
    sems = [dma((n,)), dma] + crossing + [dma]
    sems += one + one + one + one + two + one + one + one + one
    return pl.pallas_call(
        kernel,
        out_shape=jax.ShapeDtypeStruct((per, columns), bf),
        in_specs=[pl.BlockSpec(memory_space=pl.ANY)] * 3
        + [pl.BlockSpec(memory_space=pltpu.VMEM)],
        out_specs=pl.BlockSpec(memory_space=pl.ANY),
        scratch_shapes=buffers + sems,
        compiler_params=pltpu.CompilerParams(
            collective_id=0, has_side_effects=True, vmem_limit_bytes=60 * 2**20
        ),
    )(hidden, cotangent, weights, segments)


def solution(mesh):
    return jax.shard_map(
        shards,
        mesh=mesh,
        in_specs=(P("mp", "dp", "shard"), P("mp", "dp", "shard"), P("mp", "dp", "shard"), P()),
        out_specs=P(("dp", "mp"), "shard"),
        check_vma=False,
    )
```

```python
import math

import jax
import jax.numpy as jnp
from jax import lax
from jax.experimental import pallas as pl
from jax.experimental.pallas import tpu as pltpu
from jax.sharding import PartitionSpec as P

EX = 3
Y = 4
CHUNK = 256
DIRECT = 4
EARLY = 4
ROWS_AT_ONCE = 64
LAG_HALF, LAG_SUM, LAG_GRAD, LAG_PASS, LAG_RELAY = 1, 2, 4, 6, 7
LAG_FISHER, LAG_CORE, LAG_NEAR, LAG_FAR = 8, 9, 11, 12


def kernel(
    hidden, cotangent, weights, segments, out,
    w, cot, states, masked, part, half_in, part_in, own, cross, cross_in, grads, sums,
    core_in, near_in, far_in, result, fisher,
    load_sem, cot_sem, hid_ssem, hid_rsem, x_ssem, x_rsem, out_sem,
    half_ssem, half_rsem, part_ssem, part_rsem, cross_ssem, cross_rsem,
    gz_ssem, gz_rsem, gy_ssem, gy_rsem, relay_ssem, relay_rsem,
    core_ssem, core_rsem, near_ssem, near_rsem, far_ssem, far_rsem,
):
    chunks, block_rows, cw = w.shape
    tokens = cot.shape[0]
    quarter = tokens // Y
    relayed = chunks - DIRECT
    scale = 1.0 / math.sqrt(block_rows * 2 * Y)
    mp, dp, sh = lax.axis_index("mp"), lax.axis_index("dp"), lax.axis_index("shard")
    core, b0, b1 = lax.rem(mp, 2), lax.rem(mp // 2, 2), mp // 4
    zh, y = dp // Y, lax.rem(dp, Y)

    def y_peer(d):
        return {"dp": zh * Y + lax.rem(y + d, Y)}

    def x_peer(d):
        return {"shard": lax.rem(sh + d, Y)}

    z_peer = {"dp": (1 - zh) * Y + y}
    core_peer = {"mp": mp + 1 - 2 * core}
    near_peer = {"mp": mp + 2 - 4 * b0}
    far_peer = {"mp": mp + 4 - 8 * b1}

    def remote(src, dst, ssem, rsem, device):
        return pltpu.make_async_remote_copy(
            src_ref=src,
            dst_ref=dst,
            send_sem=ssem,
            recv_sem=rsem,
            device_id=device,
            device_id_type=pl.DeviceIdType.MESH,
        )

    def load_w(c):
        cols = pl.ds(pl.multiple_of(c * cw, cw), cw)
        return pltpu.make_async_copy(weights.at[0, :, cols], w.at[c], load_sem.at[c])

    load_cot = pltpu.make_async_copy(cotangent.at[0], cot, cot_sem)

    def start_loads(c, carry):
        load_w(c).start()
        return carry

    load_cot.start()
    lax.fori_loop(0, chunks, start_loads, 0)

    barrier = pltpu.get_barrier_semaphore()

    def greet(device):
        pl.semaphore_signal(
            barrier, inc=1, device_id=device, device_id_type=pl.DeviceIdType.MESH
        )

    def from_self(j):
        return jnp.logical_and(sh == dp // 2, dp == j)

    def to_self(b, q):
        return jnp.logical_and(dp == 2 * sh + b, sh == q)

    peers = [y_peer(1), y_peer(2), y_peer(3), x_peer(1), x_peer(2), x_peer(3)]
    peers += [z_peer, core_peer, near_peer, far_peer]
    for device in peers:
        greet(device)
    for j in range(2 * Y):

        @pl.when(jnp.logical_not(from_self(j)))
        def _():
            greet({"dp": j, "shard": dp // 2})

    at_home = jnp.where(sh == dp // 2, 1, 0)
    pl.semaphore_wait(barrier, len(peers) + 2 * Y - at_home)

    def hid_send(b, q):
        return remote(
            hidden.at[0, pl.ds(q * quarter, quarter), pl.ds(b * block_rows, block_rows)],
            states.at[dp, q],
            hid_ssem.at[b * Y + q],
            hid_rsem.at[dp],
            {"dp": 2 * sh + b, "shard": q},
        )

    def hid_local(b, q):
        return pltpu.make_async_copy(
            hidden.at[0, pl.ds(q * quarter, quarter), pl.ds(b * block_rows, block_rows)],
            states.at[dp, q],
            hid_ssem.at[b * Y + q],
        )

    def hid_recv(j):
        return remote(
            states.at[j, sh], states.at[j, sh], hid_ssem.at[0], hid_rsem.at[j], {"dp": j, "shard": dp // 2}
        )

    for b in range(2):
        for q in range(Y):

            @pl.when(to_self(b, q))
            def _():
                hid_local(b, q).start()

            @pl.when(jnp.logical_not(to_self(b, q)))
            def _():
                hid_send(b, q).start()

    def x_send(j, d):
        place = states.at[j, sh]
        return remote(place, place, x_ssem.at[d - 1], x_rsem.at[j // Y], x_peer(d))

    def x_forward(j):
        @pl.when(jnp.logical_not(from_self(j)))
        def _():
            hid_recv(j).wait_recv()

        @pl.when(from_self(j))
        def _():
            hid_local(lax.rem(dp, 2), sh).wait()

        for d in range(1, Y):
            x_send(j, d).start()

    for side in (zh, 1 - zh):
        for i in range(Y):
            x_forward(side * Y + i)
    def x_arrived(side):
        others = states.at[pl.ds(side * Y, Y), pl.ds(0, Y - 1)]
        remote(others, others, x_ssem.at[0], x_rsem.at[side], x_peer(1)).wait_recv()

    def products(c, side):
        def some(j, carry):
            rows = states[side * Y + j].reshape(tokens, block_rows)
            part[c, side, j] = jnp.dot(
                rows, w[c], preferred_element_type=jnp.float32
            ).astype(jnp.bfloat16)
            return carry

        lax.fori_loop(0, Y, some, 0)

    def early(c, carry):
        load_w(c).wait()
        products(c, zh)
        return carry

    x_arrived(zh)
    lax.fori_loop(0, EARLY, early, 0)
    x_arrived(1 - zh)

    half = tokens // 2

    def y_next(i):
        return lax.rem(y + (1, Y - 1)[i], Y)

    def y_to(i):
        return y_peer((1, Y - 1)[i])

    def half_send(c, i):
        return remote(
            part.at[c, :, lax.rem(y + 2, Y), pl.ds(i * half, half)], half_in.at[c, i],
            half_ssem, half_rsem.at[c], y_to(i),
        )

    def soon_send(c, i):
        rows = pl.ds((1 - i) * half, half)
        return remote(
            part.at[c, :, y_next(i), rows], part_in.at[c, i, :, rows],
            part_ssem, part_rsem.at[c], y_to(i),
        )

    def late_send(c, i):
        rows = pl.ds(i * half, half)
        return remote(
            part.at[c, :, y_next(i), rows], part_in.at[c, i, :, rows],
            part_ssem, part_rsem.at[c], y_to(i),
        )

    def cross_send(c):
        return remote(cross.at[c], cross_in.at[c], cross_ssem, cross_rsem.at[c], z_peer)

    def gz_send(c):
        place = grads.at[c, zh, y]
        return remote(place, place, gz_ssem, gz_rsem.at[c], z_peer)

    def gz_recv(c):
        place = grads.at[c, 1 - zh, y]
        return remote(place, place, gz_ssem, gz_rsem.at[c], z_peer)

    def gy_send(c, side, i):
        place = grads.at[c, side, y]
        return remote(place, place, gy_ssem, gy_rsem.at[c, side], y_to(i))

    def arrived(ref, rsem):
        remote(ref, ref, cross_ssem, rsem, z_peer).wait_recv()

    def relay_send(c, side, i):
        place = grads.at[c, side, y_next(1 - i), pl.ds(i * half, half)]
        return remote(place, place, relay_ssem, relay_rsem.at[c], y_to(i))

    def direct_send(c, side, i):
        place = grads.at[c, side, y, pl.ds(i * half, half)]
        return remote(place, place, relay_ssem, relay_rsem.at[c], y_peer(2))

    def spread(c, side):
        for i in range(2):
            gy_send(c, side, i).start()

        @pl.when(c >= relayed)
        def _():
            for i in range(2):
                direct_send(c, side, i).start()

    def core_send(c):
        return remote(
            sums.at[c, 1 - core], core_in.at[c], core_ssem, core_rsem.at[c], core_peer
        )

    def near_send(c):
        return remote(
            sums.at[c, core, 1 - b0], near_in.at[c], near_ssem, near_rsem.at[c], near_peer
        )

    def far_send(c):
        return remote(
            sums.at[c, core, b0, 1 - b1], far_in.at[c], far_ssem, far_rsem.at[c], far_peer
        )

    def store(c):
        cols = pl.ds(pl.multiple_of(c * cw, cw), cw)
        return pltpu.make_async_copy(result.at[c], out.at[:, cols], out_sem)

    def product(c):
        @pl.when(c >= EARLY)
        def _():
            early(c, 0)

        products(c, 1 - zh)
        for i in range(2):
            half_send(c, i).start()
        for i in range(2):
            soon_send(c, i).start()

    def add_half(c):
        arrived(half_in.at[c], half_rsem.at[c])
        for i in range(2):
            rows = pl.ds(i * half, half)
            part[c, :, y_next(i), rows] = (
                part[c, :, y_next(i), rows].astype(jnp.float32)
                + half_in[c, i].astype(jnp.float32)
            ).astype(jnp.bfloat16)
            late_send(c, i).start()

    def mask_states(first, last):
        def some(j, carry):
            rows = states[j].reshape(tokens, block_rows)
            turned = rows.astype(jnp.float32).T
            labels = segments[pl.ds(j, 1), :]
            for e in range(EX):
                masked[j * EX + e] = jnp.where(labels == e, turned, 0.0).astype(jnp.bfloat16)
            return carry

        lax.fori_loop(first, last, some, 0)

    def add_up(c):
        arrived(part_in.at[c], part_rsem.at[c])

        def total(side):
            acc = part[c, side, y].astype(jnp.float32)
            for i in range(2):
                acc += part_in[c, i, side].astype(jnp.float32)
            return acc

        cross[c] = total(1 - zh).astype(jnp.bfloat16)
        cross_send(c).start()
        own[c] = total(zh)

    def gradient(c):
        cross_send(c).wait_recv()
        pre = (own[c] + cross_in[c].astype(jnp.float32)) * scale
        sig = jax.nn.sigmoid(pre)
        grads[c, zh, y] = (
            cot[:, pl.ds(pl.multiple_of(c * cw, cw), cw)].astype(jnp.float32) * sig * (1.0 + pre * (1.0 - sig))
        ).astype(jnp.bfloat16)
        gz_send(c).start()
        spread(c, zh)

    def relay(c, side):
        arrived(grads.at[c, side, pl.ds(0, 2)], gy_rsem.at[c, side])

        @pl.when(c < relayed)
        def _():
            for i in range(2):
                relay_send(c, side, i).start()

    def pass_on(c):
        gz_recv(c).wait_recv()
        spread(c, 1 - zh)
        relay(c, zh)

    def relay_far(c):
        relay(c, 1 - zh)

    def fishers(c):
        arrived(grads.at[c, 0, pl.ds(0, 2)], relay_rsem.at[c])

        def some(r, carry):
            rows = pl.ds(pl.multiple_of(r * ROWS_AT_ONCE, ROWS_AT_ONCE), ROWS_AT_ONCE)
            acc = jnp.zeros((ROWS_AT_ONCE, cw), jnp.float32)
            for j in range(2 * Y):
                cols = grads[c, j // Y, j % Y]
                for e in range(EX):
                    grad = jnp.dot(
                        masked[j * EX + e, rows, :], cols, preferred_element_type=jnp.float32
                    )
                    acc += grad * grad
            fisher[rows, :] = acc
            return carry

        lax.fori_loop(0, block_rows // ROWS_AT_ONCE, some, 0)
        per = block_rows // 8
        for m in range(8):
            f = fisher[m * per : (m + 1) * per, :]
            at = sums.at[c, m % 2, (m // 2) % 2, m // 4]
            at[0] = (f * w[c, m * per : (m + 1) * per, :].astype(jnp.float32)).astype(jnp.bfloat16)
            at[1] = f.astype(jnp.bfloat16)
        core_send(c).start()

    def add_core(c):
        core_send(c).wait_recv()
        for i in (0, 1):
            side = b0 if i else 1 - b0
            sums[c, core, side] = (
                sums[c, core, side].astype(jnp.float32) + core_in[c, side].astype(jnp.float32)
            ).astype(jnp.bfloat16)
            if i == 0:
                near_send(c).start()

    def add_near(c):
        near_send(c).wait_recv()
        for i in (0, 1):
            side = b1 if i else 1 - b1
            sums[c, core, b0, side] = (
                sums[c, core, b0, side].astype(jnp.float32)
                + near_in[c, side].astype(jnp.float32)
            ).astype(jnp.bfloat16)
            if i == 0:
                far_send(c).start()

    def add_far(c):
        far_send(c).wait_recv()
        both = sums[c, core, b0, b1].astype(jnp.float32) + far_in[c].astype(jnp.float32)
        result[c] = (both[0] / both[1]).astype(jnp.bfloat16)
        store(c).start()

    stages = [
        (product, 0), (add_half, LAG_HALF), (add_up, LAG_SUM), (gradient, LAG_GRAD),
        (pass_on, LAG_PASS), (relay_far, LAG_RELAY),
        (fishers, LAG_FISHER), (add_core, LAG_CORE), (add_near, LAG_NEAR), (add_far, LAG_FAR),
    ]

    def step(t, carry):
        for stage, lag in stages:
            if lag < LAG_FISHER:
                c = t - lag

                @pl.when(jnp.logical_and(c >= 0, c < chunks))
                def _():
                    stage(c)

            else:

                def run(u, carry):
                    c = t - lag + u
                    runs = jnp.logical_and(u == 0, jnp.logical_and(c >= 0, c < relayed))
                    direct = jnp.logical_and(u == 1, jnp.logical_and(c >= relayed, c < chunks))

                    @pl.when(jnp.logical_or(runs, direct))
                    def _():
                        stage(c)

                    return carry

                lax.fori_loop(0, 2, run, 0)

        @pl.when(jnp.logical_and(t >= 1, t <= Y))
        def _():
            mask_states(2 * t - 2, 2 * t)

        return carry

    load_cot.wait()
    lax.fori_loop(0, chunks + LAG_FAR - 1, step, 0)

    for b in range(2):
        for q in range(Y):

            @pl.when(jnp.logical_not(to_self(b, q)))
            def _():
                hid_send(b, q).wait_send()

    def sent(ref, ssem):
        remote(ref, ref, ssem, cross_rsem.at[0], z_peer).wait_send()

    for i in range(1, Y):
        sent(states.at[:, 0], x_ssem.at[i - 1])
    sent(half_in, half_ssem)
    sent(part_in, part_ssem)
    sent(cross, cross_ssem)
    sent(cross, gz_ssem)
    sent(part_in, gy_ssem)
    sent(half_in, relay_ssem)
    sent(core_in, core_ssem)
    sent(near_in, near_ssem)
    sent(far_in, far_ssem)

    pltpu.make_async_copy(out, out, out_sem).wait()


def shards(hidden, cotangent, weights, segments):
    tokens, block_rows, columns = hidden.shape[1], weights.shape[1], weights.shape[2]
    cw = CHUNK
    n = columns // cw
    per = block_rows // 8
    bf, f32 = jnp.bfloat16, jnp.float32
    dma = pltpu.SemaphoreType.DMA
    buffers = [
        pltpu.VMEM((n, block_rows, cw), bf),
        pltpu.VMEM((tokens, columns), bf),
        pltpu.VMEM((2 * Y, Y, tokens // Y, block_rows), bf),
        pltpu.VMEM((2 * Y * EX, block_rows, tokens), bf),
        pltpu.VMEM((n, 2, Y, tokens, cw), bf),
        pltpu.VMEM((n, 2, 2, tokens // 2, cw), bf),
        pltpu.VMEM((n, 2, 2, tokens, cw), bf),
        pltpu.VMEM((n, tokens, cw), f32),
        pltpu.VMEM((n, tokens, cw), bf),
        pltpu.VMEM((n, tokens, cw), bf),
        pltpu.VMEM((n, 2, Y, tokens, cw), bf),
        pltpu.VMEM((n, 2, 2, 2, 2, per, cw), bf),
        pltpu.VMEM((n, 2, 2, 2, per, cw), bf),
        pltpu.VMEM((n, 2, 2, per, cw), bf),
        pltpu.VMEM((n, 2, per, cw), bf),
        pltpu.VMEM((n, per, cw), bf),
        pltpu.VMEM((block_rows, cw), f32),
    ]
    one, two = [dma, dma((n,))], [dma, dma((n, 2))]
    crossing = [dma((2 * Y,))] * 2 + [dma((Y - 1,)), dma((2,))]
    sems = [dma((n,)), dma] + crossing + [dma]
    sems += one + one + one + one + two + one + one + one + one
    return pl.pallas_call(
        kernel,
        out_shape=jax.ShapeDtypeStruct((per, columns), bf),
        in_specs=[pl.BlockSpec(memory_space=pl.ANY)] * 3
        + [pl.BlockSpec(memory_space=pltpu.VMEM)],
        out_specs=pl.BlockSpec(memory_space=pl.ANY),
        scratch_shapes=buffers + sems,
        compiler_params=pltpu.CompilerParams(
            collective_id=0, has_side_effects=True, vmem_limit_bytes=60 * 2**20
        ),
    )(hidden, cotangent, weights, segments)


def solution(mesh):
    return jax.shard_map(
        shards,
        mesh=mesh,
        in_specs=(P("mp", "dp", "shard"), P("mp", "dp", "shard"), P("mp", "dp", "shard"), P()),
        out_specs=P(("dp", "mp"), "shard"),
        check_vma=False,
    )
```
